128 devices in a mesh: set: 16 (over x, z), lev: 8 (over y, core).
Axes of the slice: x: 4, y: 4, z: 4, core: 2. Of those that a mesh axis runs over, the one named last changes fastest.
Arguments:
- spectral: bfloat16 [2, 128, 2, 640, 1281], P(None, None, None, ('set', 'lev')), may hold values from -0.0048828125 to 0.0048828125
- vertical: bfloat16 [2, 128, 128], P(None, 'lev'), may hold values from -0.5 to 0.5
- value_table: bfloat16 [640, 1281, 128], P(('set', 'lev')), may hold values from -6 to 6
- slope_table: bfloat16 [640, 1281, 128], P(('set', 'lev')), may hold values from -6 to 6
- wave_low: int32 [640], P(('set', 'lev')), may hold values from 0 to 639, each once
- lat_slot: int32 [128], replicated, may hold values from 0 to 127, each once
- lon_counts: int32 [128], replicated, may hold values from 20 to 5136, as said below
Outputs:
- fields: bfloat16 [2, 128, 128, 1024], P(None, 'lev', 'set')
- slopes: bfloat16 [2, 128, 128, 1024], P(None, 'lev', 'set')
The draws below stay inside these ranges and needn't reach their ends.
Inputs may be any that keep to these rules, and one draw needn't show every extreme that they name: `wave_low`: A permutation; pair slot p holds zonal wavenumbers wave_low[p] and 1279 - wave_low[p], so every wavenumber from 0 to 1279 appears once. `lat_slot`: A permutation of the window's latitudes. `lon_counts`: each count is 4 i + 16 for an octahedral latitude number i from 1 to 1280; the largest count is reached in every draw.
All inputs are finite; a program needn't handle non-finite values.
Results may differ from the reference program's by a relative error of at most 0.0062.
Values may be sent and summed in bfloat16 or wider, within the bound.
A program may use at most 128 MiB of HBM per device.

```python
import jax
import jax.numpy as jnp
from jax import lax

TRUNC = 1279
PAIRS = 640
LEVELS = 128
LAT = 128
LONS = 1024


def draw_lon_counts(key, part):
    key = jax.random.fold_in(key, 11)
    key_rows, key_top = jax.random.split(key)
    number = jax.random.randint(key_rows, (LAT,), 1, TRUNC + 2)
    where_top = jax.random.randint(key_top, (), 0, LAT)
    number = jnp.where(jnp.arange(LAT) == where_top, TRUNC + 1, number)
    return (4 * number + 16).astype(jnp.int32)


def steps_of(own_key, shape, cuts, least, largest):
    level, own = 1.0, jax.random.fold_in(own_key, 6)
    for dim, parts in cuts:
        draws = jnp.exp(jax.random.uniform(jax.random.fold_in(own, dim), (parts,), jnp.float32, least / len(cuts), largest / len(cuts)))
        level = level * jnp.repeat(draws, shape[dim] // parts).reshape([-1 if axis == dim else 1 for axis in range(len(shape))])
    return level


def gaussian(stream_key, shape, spread, reach, shards=(), held_as=jnp.bfloat16):
    drawn = jax.random.normal(stream_key, shape, jnp.float32) * spread
    if len(shards) > 0:
        drawn = steps_of(stream_key, shape, shards, -0.22, 0.18) * drawn
    return jnp.clip(drawn, min=-reach, max=reach).astype(held_as)


def setup_inputs(seed: int = 0) -> dict:
    arg_keys = jax.random.split(jax.random.key(seed), 8)
    spectral = gaussian(arg_keys[0], (2, LEVELS, 2, PAIRS, TRUNC + 2), ((TRUNC + 1) * (TRUNC + 1)) ** -0.5, 0.0048828125, ((3, 128),))
    vertical = gaussian(arg_keys[1], (2, LEVELS, LEVELS), LEVELS ** -0.5, 0.5, ((1, 8),))
    value_table = gaussian(arg_keys[2], (PAIRS, TRUNC + 2, LAT), 1.0, 6.0, ((0, 128),))
    slope_table = gaussian(arg_keys[3], (PAIRS, TRUNC + 2, LAT), 1.0, 6.0, ((0, 128),))
    wave_low = jax.random.permutation(arg_keys[4], PAIRS).astype(jnp.int32)
    lat_slot = jax.random.permutation(arg_keys[5], LAT).astype(jnp.int32)
    lon_counts = draw_lon_counts(jax.random.fold_in(arg_keys[7], 71), 0)
    return {"spectral": spectral, "vertical": vertical, "value_table": value_table, "slope_table": slope_table, "wave_low": wave_low, "lat_slot": lat_slot, "lon_counts": lon_counts}


two_pi = 6.283185307179586


def degree_scale(low_waves, top_degree, pair_rows):
    column = jnp.arange(pair_rows, dtype=jnp.int32)
    is_low = column[None, :] <= (top_degree - low_waves)[:, None]
    degree = jnp.where(is_low, low_waves[:, None] + column[None, :], column[None, :] - 1)
    implicit_scale = (degree * (degree + 1)).astype(jnp.float32) / jnp.float32(top_degree * (top_degree + 1))
    return is_low, implicit_scale


def longitude_table(wavenumbers, lon_count, columns):
    column = jnp.arange(columns, dtype=jnp.int32)
    product = (wavenumbers[:, None] * column[None, :]) % lon_count
    phase_angle = product.astype(jnp.float32) * (two_pi / lon_count.astype(jnp.float32))
    weight = jnp.where(wavenumbers == 0, 1.0, 2.0).astype(jnp.float32)[:, None]
    inside = (column < lon_count)[None, :]
    cosine = jnp.where(inside, weight * jnp.cos(phase_angle), 0.0)
    sine_part = jnp.where(inside, -weight * jnp.sin(phase_angle), 0.0)
    return jnp.concatenate([cosine, sine_part], axis=0).astype(jnp.bfloat16)


def reference(spectral, vertical, value_table, slope_table, wave_low, lat_slot, lon_counts):
    pair_rows = TRUNC + 2
    is_low, implicit_scale = degree_scale(wave_low, TRUNC, pair_rows)
    matrices = vertical.astype(jnp.float32)
    by_pair = jnp.moveaxis(spectral, 3, 0)

    def one_pair(inputs):
        coeffs, table_value, table_slope, low_rows, pair_scale = inputs
        widened = coeffs.astype(jnp.float32)
        coupled = jnp.einsum("flk,fkrj->flrj", matrices, widened)
        adjusted = (widened + pair_scale * coupled).astype(jnp.bfloat16)
        low_keep = low_rows.astype(jnp.bfloat16)
        high_keep = jnp.logical_not(low_rows).astype(jnp.bfloat16)
        halves = jnp.stack([adjusted * low_keep, adjusted * high_keep]).reshape(-1, pair_rows)
        band_value = jnp.dot(halves, table_value, preferred_element_type=jnp.float32).astype(jnp.bfloat16)
        band_slope = jnp.dot(halves, table_slope, preferred_element_type=jnp.float32).astype(jnp.bfloat16)
        return jnp.stack([band_value, band_slope])

    band_all = lax.map(one_pair, (by_pair, value_table, slope_table, is_low, implicit_scale))
    band_all = band_all.reshape(PAIRS, 2, 2, 2, LEVELS, 2, LAT)
    wavenumbers = jnp.stack([wave_low, TRUNC - wave_low], axis=-1).reshape(-1)

    def one_slot(slot_index):
        latitude = lat_slot[slot_index]
        lon_count = lon_counts[latitude]
        column = lax.dynamic_index_in_dim(band_all, latitude, axis=6, keepdims=False)
        matrix = jnp.transpose(column, (3, 1, 4, 5, 0, 2)).reshape(4 * LEVELS, 2 * (TRUNC + 1))
        lon_table = longitude_table(wavenumbers, lon_count, LONS)
        result = jnp.dot(matrix, lon_table, preferred_element_type=jnp.float32).astype(jnp.bfloat16)
        return result.reshape(2, 2, LEVELS, LONS)

    gridded = lax.map(one_slot, jnp.arange(LAT, dtype=jnp.int32))
    fields = jnp.transpose(gridded[:, :, 0], (1, 2, 0, 3))
    slopes = jnp.transpose(gridded[:, :, 1], (1, 2, 0, 3))
    return fields, slopes
```

```python
import functools

import jax
import jax.numpy as jnp
from jax import lax
from jax.experimental import pallas as pl
from jax.experimental.pallas import tpu as pltpu
from jax.sharding import PartitionSpec as P

TRUNC = 1279
ROWS = 1281
PAIRS = 5
SETS = 16
LEVS = 8
SLOTS = 8
LONS = 1024
PAD = 1408
BLK = 128
HIGH0 = 640
MESH = pl.DeviceIdType.MESH
F32 = jnp.float32
BF16 = jnp.bfloat16


def iota(shape, dim):
    return lax.broadcasted_iota(jnp.int32, shape, dim)


def turn(x, count, inverse):
    r = x - jnp.floor(x * inverse + 0.5) * count
    t = r * inverse * 3.14159265358979
    t2 = t * t
    sn = t * (1.0 + t2 * (-1 / 6 + t2 * (1 / 120 + t2 * (-1 / 5040 + t2 * (1 / 362880 - t2 * (1 / 39916800))))))
    cs = 1.0 + t2 * (-1 / 2 + t2 * (1 / 24 + t2 * (-1 / 720 + t2 * (1 / 40320 - t2 * (1 / 3628800)))))
    return 1.0 - 2.0 * sn * sn, 2.0 * sn * cs


def kernel(
    spec, vert, tabs_v, tabs_s, wave, lat, counts, lat_row,
    out_f, out_s,
    sbuf, tbuf, tpt, place, abuf, adjf, xbuf, rbuf, dbuf, vall, vt,
    wave_me, wave_set, wave_pack, wave_all, wcol, cval, cinv, psi_c, psi_s,
    table, acc, df, outf, outb,
    sem_s, sem_t, sem_v, sem_w1, sem_w2, sem_send1, sem_recv1, sem_send2, sem_recv2, sem_loc, sem_out,
):
    a = lax.axis_index("set")
    b = lax.axis_index("lev")

    def nth_set(i):
        return lax.rem(a + i, SETS)

    def nth_lev(i):
        return lax.rem(b + i, LEVS)

    def load_tables(p):
        return (
            pltpu.make_async_copy(tabs_v.at[p], tbuf.at[0, p], sem_t.at[0, p]),
            pltpu.make_async_copy(tabs_s.at[p], tbuf.at[1, p], sem_t.at[1, p]),
        )

    def load_spec(p):
        return [
            pltpu.make_async_copy(spec.at[f, p], sbuf.at[f, p, pl.ds(0, ROWS)], sem_s.at[f, p]) for f in range(2)
        ]

    for p in range(PAIRS):
        for c in load_tables(p):
            c.start()
    for p in range(PAIRS):
        for c in load_spec(p):
            c.start()
    own_v = pltpu.make_async_copy(vert, vall.at[b], sem_v.at[2])
    own_v.start()

    bar = pltpu.get_barrier_semaphore()

    @pl.loop(1, LEVS)
    def _(i):
        pl.semaphore_signal(bar, inc=1, device_id=(a, nth_lev(i)), device_id_type=MESH)

    @pl.loop(1, SETS)
    def _(i):
        pl.semaphore_signal(bar, inc=1, device_id=(nth_set(i), b), device_id_type=MESH)

    for f in range(2):
        for p in range(PAIRS):
            sbuf[f, p, ROWS:PAD] = jnp.zeros((PAD - ROWS, 2, 128), BF16)

    lane = iota((8, 128), 1)
    row_of_waves = jnp.zeros((8, 128), F32)
    for p in range(PAIRS):
        row_of_waves = jnp.where(lane == p, wave[p].astype(F32), row_of_waves)
    wave_me[...] = row_of_waves

    sub = iota((8, 128), 0)
    cv = jnp.zeros((8, 128), F32)
    for s in range(SLOTS):
        c_s = counts[lat[a * SLOTS + s]].astype(F32)
        cv = jnp.where(sub == s, c_s, cv)
    cval[...] = cv
    cinv[...] = 1.0 / cv
    for t in range(LONS // 128):
        x = ((iota((8, 128), 1) + t * 128) * TRUNC).astype(F32)
        pc, ps = turn(x, cval[...], cinv[...])
        psi_c[:, t * 128 : t * 128 + 128] = pc
        psi_s[:, t * 128 : t * 128 + 128] = ps

    @pl.loop(0, 8)
    def _(i):
        row = iota((128, 1024), 0)
        col = iota((128, 1024), 1)
        h, f, r = i // 4, (i // 2) % 2, i % 2
        want = (row // 16) * 128 + h * 64 + r * 32 + f * 16 + row % 16
        place[pl.ds(pl.multiple_of(i * 128, 128), 128), :] = jnp.where(col == want, 1.0, 0.0).astype(BF16)

    r_row = iota((256, 128), 0)
    pick = jnp.where(iota((256, 128), 1) == (r_row // 16) * 8 + r_row % 8, 1.0, 0.0).astype(BF16)
    lat_b = jnp.broadcast_to(lat_row[...], (128, 128)).astype(F32).astype(BF16)
    lat_col = lax.dot_general(pick, lat_b, (((1,), (1,)), ((), ())), preferred_element_type=F32)
    hit = lat_col == iota((256, 128), 1).astype(F32)
    k_row = (r_row // 8) % 2
    order = jnp.concatenate(
        [
            jnp.where(jnp.logical_and(hit, k_row == 0), 1.0, 0.0),
            jnp.where(jnp.logical_and(hit, k_row == 1), 1.0, 0.0),
        ],
        axis=1,
    ).astype(BF16)

    @pl.loop(0, PAIRS)
    def _(p):
        for c in load_tables(p):
            c.wait()

        @pl.loop(0, 5)
        def _(t):
            j0 = pl.multiple_of(t * 256, 256)
            both = jnp.concatenate([tbuf[0, p, pl.ds(j0, 256)], tbuf[1, p, pl.ds(j0, 256)]], axis=1)
            turned = lax.dot_general(order, both, (((1,), (1,)), ((), ())), preferred_element_type=F32)
            tpt[p, :, pl.ds(j0, 256)] = turned.astype(BF16)

        last = jnp.concatenate([tbuf[0, p, 1280:1281], tbuf[1, p, 1280:1281]], axis=1).astype(F32)
        last = jnp.broadcast_to(last, (128, 256))
        last = jnp.where(iota((128, 256), 0) == 0, last, 0.0).astype(BF16)
        turned = lax.dot_general(order, last, (((1,), (1,)), ((), ())), preferred_element_type=F32)
        tpt[p, :, 1280:PAD] = turned.astype(BF16)

    own_v.wait()
    pl.semaphore_wait(bar, LEVS - 1 + SETS - 1)

    @pl.loop(1, LEVS)
    def _(i):
        pltpu.make_async_remote_copy(
            src_ref=vall.at[b], dst_ref=vall.at[b], send_sem=sem_v.at[0], recv_sem=sem_v.at[1],
            device_id=(a, nth_lev(i)), device_id_type=MESH,
        ).start()

    @pl.loop(1, SETS)
    def _(i):
        pltpu.make_async_remote_copy(
            src_ref=wave_me, dst_ref=wave_set.at[a], send_sem=sem_w1.at[0], recv_sem=sem_w1.at[1],
            device_id=(nth_set(i), b), device_id_type=MESH,
        ).start()

    for e in range(2):
        pltpu.make_async_copy(vall.at[pl.ds(0, LEVS - 1)], vall.at[pl.ds(0, LEVS - 1)], sem_v.at[e]).wait()
    for f in range(2):
        vt[f] = vall[:, f].reshape(128, 128).astype(F32).T.astype(BF16)

    def send1(p):
        pltpu.make_async_copy(xbuf.at[p, a], rbuf.at[p, a], sem_loc.at[0, p]).start()

        @pl.loop(1, SETS)
        def _(i):
            t = nth_set(i)
            pltpu.make_async_remote_copy(
                src_ref=xbuf.at[p, t], dst_ref=rbuf.at[p, a], send_sem=sem_send1.at[p], recv_sem=sem_recv1.at[p],
                device_id=(t, b), device_id_type=MESH,
            ).start()

    def send2(p):
        pltpu.make_async_copy(xbuf.at[p, a], rbuf.at[p, a], sem_loc.at[0, p]).wait()
        pltpu.make_async_copy(
            xbuf.at[p, pl.ds(0, SETS - 1)], rbuf.at[p, pl.ds(0, SETS - 1)], sem_recv1.at[p]
        ).wait()
        pltpu.make_async_copy(rbuf.at[p, :, b], dbuf.at[p, b], sem_loc.at[1, p]).start()

        @pl.loop(1, LEVS)
        def _(i):
            t = nth_lev(i)
            pltpu.make_async_remote_copy(
                src_ref=rbuf.at[p, :, t], dst_ref=dbuf.at[p, b], send_sem=sem_send2.at[p], recv_sem=sem_recv2.at[p],
                device_id=(a, t), device_id_type=MESH,
            ).start()

    def wait2(p):
        pltpu.make_async_copy(rbuf.at[p, :, b], dbuf.at[p, b], sem_loc.at[1, p]).wait()
        pltpu.make_async_copy(
            dbuf.at[p, pl.ds(0, LEVS - 1)], dbuf.at[p, pl.ds(0, LEVS - 1)], sem_recv2.at[p]
        ).wait()

    def waits_of_sends(p):
        pltpu.make_async_copy(
            xbuf.at[p, pl.ds(0, SETS - 1)], rbuf.at[p, pl.ds(0, SETS - 1)], sem_send1.at[p]
        ).wait()
        pltpu.make_async_copy(
            dbuf.at[p, pl.ds(0, LEVS - 1)], dbuf.at[p, pl.ds(0, LEVS - 1)], sem_send2.at[p]
        ).wait()

    def legendre(p):
        m = wave[p]
        for c in load_spec(p):
            c.wait()

        @pl.loop(0, PAD // BLK)
        def _(t):
            j0 = pl.multiple_of(t * BLK, BLK)
            j = iota((2 * BLK, 128), 0) // 2 + j0
            degree = jnp.where(j <= TRUNC - m, m + j, j - 1)
            scale = (degree * (degree + 1)).astype(F32) * (1.0 / (TRUNC * (TRUNC + 1)))
            for f in range(2):
                x = sbuf[f, p, pl.ds(j0, BLK)].reshape(2 * BLK, 128)
                coupled = jnp.dot(x, vt[f], preferred_element_type=F32)
                adjf[f] = x.astype(F32) + scale * coupled
                for r in range(2):
                    abuf[pl.ds(j0, BLK), (2 * f + r) * 128 : (2 * f + r + 1) * 128] = adjf[
                        f, pl.ds(r, BLK, stride=2), :
                    ].astype(BF16)

        w_low = jnp.where(m == 0, 1.0, 2.0)
        jl = iota((256, HIGH0), 1) + HIGH0
        edge = tpt[p, :, HIGH0:1280].astype(F32)
        low_hi = jnp.where(jl <= TRUNC - m, edge * w_low, 0.0).astype(BF16)
        low = jnp.dot(
            (tpt[p, :, 0:HIGH0].astype(F32) * w_low).astype(BF16), abuf[0:HIGH0, :], preferred_element_type=F32
        )
        low = low + jnp.dot(low_hi, abuf[HIGH0:1280, :], preferred_element_type=F32)
        jh = iota((256, PAD - HIGH0), 1) + HIGH0
        keep = jnp.logical_and(jh > TRUNC - m, jh < ROWS)
        high_t = jnp.where(keep, tpt[p, :, HIGH0:PAD].astype(F32) * 2.0, 0.0).astype(BF16)
        high = jnp.dot(high_t, abuf[HIGH0:PAD, :], preferred_element_type=F32)
        band = jnp.concatenate([low.astype(BF16), high.astype(BF16)], axis=1)
        for q in range(4):
            placed = jnp.dot(band, place[:, q * 256 : q * 256 + 256], preferred_element_type=F32).astype(BF16)
            for e in range(2):
                for s in range(SETS):
                    xbuf[p, s, 2 * q + e] = placed[16 * s : 16 * s + 16, 128 * e : 128 * e + 128]

    def pass_waves():
        for e in range(2):
            pltpu.make_async_copy(
                wave_set.at[pl.ds(0, SETS - 1)], wave_set.at[pl.ds(0, SETS - 1)], sem_w1.at[e]
            ).wait()
        wave_set[a] = wave_me[...]
        packed = wave_set[:, 0, :]
        wave_pack[...] = packed
        wave_all[b] = packed

        @pl.loop(1, LEVS)
        def _(i):
            pltpu.make_async_remote_copy(
                src_ref=wave_pack, dst_ref=wave_all.at[b], send_sem=sem_w2.at[0], recv_sem=sem_w2.at[1],
                device_id=(a, nth_lev(i)), device_id_type=MESH,
            ).start()

    @pl.loop(0, PAIRS)
    def _(p):
        legendre(p)
        send1(p)

        @pl.when(p == 0)
        def _():
            pass_waves()

        @pl.when(p >= 2)
        def _():
            send2(p - 2)

    for e in range(2):
        pltpu.make_async_copy(
            wave_all.at[pl.ds(0, LEVS - 1)], wave_all.at[pl.ds(0, LEVS - 1)], sem_w2.at[e]
        ).wait()

    def tables(p):
        waves = wave_all[...].reshape(128, 128)
        mine = jnp.sum(jnp.where(iota((128, 128), 1) == p, waves, 0.0), axis=1, keepdims=True)
        wcol[...] = jnp.broadcast_to(mine, (128, 128))

        @pl.loop(0, SLOTS)
        def _(s):
            count = cval[pl.ds(s, 1), :]
            inverse = cinv[pl.ds(s, 1), :]
            for g in range(4):
                rows = slice(32 * g, 32 * g + 32)
                m = wcol[rows, :]
                c, n = turn(m * iota((32, 128), 1).astype(F32), count, inverse)
                sc, sn = turn(m * 128.0, count, inverse)
                for t in range(LONS // 128):
                    table[p, s, rows, 128 * t : 128 * t + 128] = c.astype(BF16)
                    table[p, s, 128 + 32 * g : 160 + 32 * g, 128 * t : 128 * t + 128] = n.astype(BF16)
                    if t < LONS // 128 - 1:
                        c, n = c * sc - n * sn, n * sc + c * sn

    @pl.loop(0, PAIRS)
    def _(p):
        tables(p)

        @pl.when(p == 0)
        def _():
            send2(3)

        @pl.when(p == 2)
        def _():
            send2(4)

    def sums(p, s):
        cos_rows, sin_rows = [[], [], []], [[], [], []]
        for k in range(2):
            x = df[pl.ds(k * 8 + s, 128, stride=16), :].T
            re0, im0, re1, im1 = x[0:32], x[32:64], x[64:96], x[96:128]
            for g, v in enumerate((re0, re1, -im1)):
                cos_rows[g].append(v)
            for g, v in enumerate((-im0, im1, re1)):
                sin_rows[g].append(v)
        cos_side = jnp.concatenate(cos_rows[0] + cos_rows[1] + cos_rows[2], axis=0)
        sin_side = jnp.concatenate(sin_rows[0] + sin_rows[1] + sin_rows[2], axis=0)
        both = jnp.concatenate([cos_side, sin_side], axis=1).astype(BF16)
        return lambda t: jnp.dot(both, table[p, s, :, 256 * t : 256 * t + 256], preferred_element_type=F32)

    @pl.loop(0, PAIRS)
    def _(p):
        wait2(p)
        df[...] = dbuf[p].reshape(2048, 128).astype(F32)

        @pl.loop(0, SLOTS)
        def _(s):
            part = sums(p, s)

            @pl.when(p == 0)
            def _():
                for t in range(4):
                    acc[s, :, 256 * t : 256 * t + 256] = part(t)

            @pl.when(jnp.logical_and(p > 0, p < PAIRS - 1))
            def _():
                for t in range(4):
                    acc[s, :, 256 * t : 256 * t + 256] += part(t)

            @pl.when(p == PAIRS - 1)
            def _():
                for t in range(4):
                    cols = slice(256 * t, 256 * t + 256)
                    total = acc[s, :, cols] + part(t)
                    pc = psi_c[pl.ds(s, 1), cols]
                    ps = psi_s[pl.ds(s, 1), cols]
                    o = total[0:64] + pc * total[64:128] + ps * total[128:192]
                    lon = (iota((64, 256), 1) + 256 * t).astype(F32)
                    count = jnp.concatenate([cval[pl.ds(s, 1), :]] * 2, axis=1)
                    o = jnp.where(lon < count, o, 0.0)
                    for e in range(2):
                        outf[2 * t + e, pl.ds(s, 64, stride=8), :] = o[:, 128 * e : 128 * e + 128]

    for t in range(8):
        outb[:, :, :, :, 128 * t : 128 * t + 128] = outf[t].reshape(2, 2, 16, 8, 128).astype(BF16)
    done = [
        pltpu.make_async_copy(outb.at[0], out_f, sem_out.at[0]),
        pltpu.make_async_copy(outb.at[1], out_s, sem_out.at[1]),
    ]
    for c in done:
        c.start()

    @pl.loop(0, PAIRS)
    def _(p):
        waits_of_sends(p)

    for c in done:
        c.wait()


def body(spectral, vertical, value_table, slope_table, wave_low, lat_slot, lon_counts):
    rows_first = jnp.transpose(spectral, (0, 3, 4, 2, 1))
    anywhere = pl.BlockSpec(memory_space=pl.ANY)
    scalars = pl.BlockSpec(memory_space=pltpu.SMEM)
    dma = pltpu.SemaphoreType.DMA
    out = jax.ShapeDtypeStruct((2, 16, SLOTS, LONS), BF16)
    return pl.pallas_call(
        kernel,
        out_shape=(out, out),
        in_specs=[anywhere] * 4 + [scalars] * 3 + [pl.BlockSpec(memory_space=pltpu.VMEM)],
        out_specs=(anywhere, anywhere),
        scratch_shapes=[
            pltpu.VMEM((2, PAIRS, PAD, 2, 128), BF16),
            pltpu.VMEM((2, PAIRS, ROWS, 128), BF16),
            pltpu.VMEM((PAIRS, 256, PAD), BF16),
            pltpu.VMEM((1024, 1024), BF16),
            pltpu.VMEM((PAD, 512), BF16),
            pltpu.VMEM((2, 2 * BLK, 128), F32),
            pltpu.VMEM((PAIRS, SETS, LEVS, 16, 128), BF16),
            pltpu.VMEM((PAIRS, SETS, LEVS, 16, 128), BF16),
            pltpu.VMEM((PAIRS, LEVS, SETS, 16, 128), BF16),
            pltpu.VMEM((LEVS, 2, 16, 128), BF16),
            pltpu.VMEM((2, 128, 128), BF16),
            pltpu.VMEM((8, 128), F32),
            pltpu.VMEM((SETS, 8, 128), F32),
            pltpu.VMEM((SETS, 128), F32),
            pltpu.VMEM((LEVS, SETS, 128), F32),
            pltpu.VMEM((128, 128), F32),
            pltpu.VMEM((8, 128), F32),
            pltpu.VMEM((8, 128), F32),
            pltpu.VMEM((8, LONS), F32),
            pltpu.VMEM((8, LONS), F32),
            pltpu.VMEM((PAIRS, SLOTS, 256, LONS), BF16),
            pltpu.VMEM((SLOTS, 192, LONS), F32),
            pltpu.VMEM((2048, 128), F32),
            pltpu.VMEM((8, 512, 128), F32),
            pltpu.VMEM((2, 2, 16, SLOTS, LONS), BF16),
            dma((2, PAIRS)),
            dma((2, PAIRS)),
            dma((3,)),
            dma((2,)),
            dma((2,)),
            dma((PAIRS,)),
            dma((PAIRS,)),
            dma((PAIRS,)),
            dma((PAIRS,)),
            dma((2, PAIRS)),
            dma((2,)),
        ],
        compiler_params=pltpu.CompilerParams(
            collective_id=0, has_side_effects=True, vmem_limit_bytes=62 * 2**20
        ),
    )(
        rows_first, vertical, value_table, slope_table, wave_low, lat_slot, lon_counts,
        lat_slot.reshape(1, 128),
    )


def solution(mesh):
    placed = (
        P(None, None, None, ("set", "lev"), None),
        P(None, "lev", None),
        P(("set", "lev"), None, None),
        P(("set", "lev"), None, None),
        P(("set", "lev")),
        P(),
        P(),
    )
    return jax.shard_map(
        body,
        mesh=mesh,
        in_specs=placed,
        out_specs=(P(None, "lev", "set", None), P(None, "lev", "set", None)),
        check_vma=False,
    )
```

```python
import functools

import jax
import jax.numpy as jnp
from jax import lax
from jax.experimental import pallas as pl
from jax.experimental.pallas import tpu as pltpu
from jax.sharding import PartitionSpec as P

TRUNC = 1279
ROWS = 1281
PAIRS = 5
SETS = 16
LEVS = 8
SLOTS = 8
LONS = 1024
SPAN = 512
PAD = 1408
BLK = 352
HIGH0 = 640
MESH = pl.DeviceIdType.MESH
F32 = jnp.float32
BF16 = jnp.bfloat16


def iota(shape, dim):
    return lax.broadcasted_iota(jnp.int32, shape, dim)


def turn(x, count, inverse):
    t = x * inverse
    t = (x - jnp.floor(t + 0.5) * count) * inverse
    t2 = t * t
    sn = t * (3.141590284 + t2 * (-5.167407698 + t2 * (2.544020811 + t2 * (-0.559489909))))
    cs = 0.999993295 + t2 * (-4.933938015 + t2 * (4.041283824 + t2 * (-1.222127058)))
    return 1.0 - 2.0 * sn * sn, 2.0 * sn * cs


def kernel(
    spec, vert, tabs_v, tabs_s, wave, lat, counts, lat_row,
    out_f, out_s,
    sbuf, slast, tbuf, tpt, place, abuf, adjf, xbuf, ra, rb, dbuf, vall, vt,
    wave_me, wave_set, wave_pack, wave_all, wcol, wave_t, shift, step, clane, cval, cinv, psi_c, psi_s,
    table, lhs, acc, df, outf, outb,
    sem_s, sem_t, sem_v, sem_w1, sem_w2, sem_a1, sem_b1, sem_a2, sem_b2, sem_loc, sem_out,
):
    a = lax.axis_index("set")
    b = lax.axis_index("lev")
    y, core = b // 2, lax.rem(b, 2)

    def nth_set(i):
        return lax.rem(a + i, SETS)

    def nth_lev(i):
        return lax.rem(b + i, LEVS)

    def load_tables(p):
        return (
            pltpu.make_async_copy(tabs_v.at[p], tbuf.at[0, p], sem_t.at[0, p]),
            pltpu.make_async_copy(tabs_s.at[p], tbuf.at[1, p], sem_t.at[1, p]),
        )

    def load_spec(p):
        whole = [
            pltpu.make_async_copy(
                spec.at[f, p, pl.ds(0, 1280)].reshape(2560, 128), sbuf.at[f, p, pl.ds(0, 2560)], sem_s.at[f, p]
            )
            for f in range(2)
        ]
        tail = [
            pltpu.make_async_copy(spec.at[f, p, pl.ds(1280, 1)], slast.at[f, p], sem_s.at[2 + f, p]) for f in range(2)
        ]
        return whole + tail

    for p in range(PAIRS):
        for c in load_tables(p):
            c.start()
    for p in range(PAIRS):
        for c in load_spec(p):
            c.start()
    own_v = pltpu.make_async_copy(vert, vall.at[b], sem_v.at[2])
    own_v.start()

    bar = pltpu.get_barrier_semaphore()

    @pl.loop(1, LEVS)
    def _(i):
        pl.semaphore_signal(bar, inc=1, device_id=(a, nth_lev(i)), device_id_type=MESH)

    @pl.loop(1, SETS)
    def _(i):
        pl.semaphore_signal(bar, inc=1, device_id=(nth_set(i), b), device_id_type=MESH)

    for f in range(2):
        for p in range(PAIRS):
            sbuf[f, p, 2576 : 2 * PAD] = jnp.zeros((2 * PAD - 2576, 128), BF16)

    lane = iota((8, 128), 1)
    row_of_waves = jnp.zeros((8, 128), F32)
    for p in range(PAIRS):
        row_of_waves = jnp.where(lane == p, wave[p].astype(F32), row_of_waves)
    wave_me[...] = row_of_waves

    sub = iota((8, 128), 0)
    cv = jnp.zeros((8, 128), F32)
    for s in range(SLOTS):
        c_s = counts[lat[a * SLOTS + s]].astype(F32)
        cv = jnp.where(sub == s, c_s, cv)
    cval[...] = cv
    clane_row = jnp.ones((1, 128), F32)
    for s in range(SLOTS):
        c_s = counts[lat[a * SLOTS + s]].astype(F32)
        clane_row = jnp.where(iota((1, 128), 1) == s, c_s, clane_row)
    clane[0:1, :] = clane_row
    clane[1:2, :] = 1.0 / clane_row
    cinv[...] = 1.0 / cv
    for t in range(LONS // 128):
        x = ((iota((8, 128), 1) + t * 128) * TRUNC).astype(F32)
        pc, ps = turn(x, cval[...], cinv[...])
        psi_c[:, t * 128 : t * 128 + 128] = pc
        psi_s[:, t * 128 : t * 128 + 128] = ps

    @pl.loop(0, 8)
    def _(i):
        row = iota((128, 1024), 0)
        col = iota((128, 1024), 1)
        h, f, r = i // 4, (i // 2) % 2, i % 2
        want = (row // 16) * 128 + h * 64 + r * 32 + f * 16 + row % 16
        place[pl.ds(pl.multiple_of(i * 128, 128), 128), :] = jnp.where(col == want, 1.0, 0.0).astype(BF16)

    r_row = iota((256, 128), 0)
    pick = jnp.where(iota((256, 128), 1) == (r_row // 16) * 8 + r_row % 8, 1.0, 0.0).astype(BF16)
    lat_b = jnp.broadcast_to(lat_row[...], (128, 128)).astype(F32).astype(BF16)
    lat_col = lax.dot_general(pick, lat_b, (((1,), (1,)), ((), ())), preferred_element_type=F32)
    hit = lat_col == iota((256, 128), 1).astype(F32)
    k_row = (r_row // 8) % 2
    order = jnp.concatenate(
        [
            jnp.where(jnp.logical_and(hit, k_row == 0), 1.0, 0.0),
            jnp.where(jnp.logical_and(hit, k_row == 1), 1.0, 0.0),
        ],
        axis=1,
    ).astype(BF16)

    @pl.loop(0, PAIRS)
    def _(p):
        for c in load_tables(p):
            c.wait()

        @pl.loop(0, 5)
        def _(t):
            j0 = pl.multiple_of(t * 256, 256)
            both = jnp.concatenate([tbuf[0, p, pl.ds(j0, 256)], tbuf[1, p, pl.ds(j0, 256)]], axis=1)
            turned = lax.dot_general(order, both, (((1,), (1,)), ((), ())), preferred_element_type=F32)
            tpt[p, :, pl.ds(j0, 256)] = turned.astype(BF16)

        last = jnp.concatenate([tbuf[0, p, 1280:1281], tbuf[1, p, 1280:1281]], axis=1).astype(F32)
        last = jnp.broadcast_to(last, (128, 256))
        last = jnp.where(iota((128, 256), 0) == 0, last, 0.0).astype(BF16)
        turned = lax.dot_general(order, last, (((1,), (1,)), ((), ())), preferred_element_type=F32)
        tpt[p, :, 1280:PAD] = turned.astype(BF16)

    own_v.wait()
    pl.semaphore_wait(bar, LEVS - 1 + SETS - 1)

    @pl.loop(1, LEVS)
    def _(i):
        pltpu.make_async_remote_copy(
            src_ref=vall.at[b], dst_ref=vall.at[b], send_sem=sem_v.at[0], recv_sem=sem_v.at[1],
            device_id=(a, nth_lev(i)), device_id_type=MESH,
        ).start()

    @pl.loop(1, SETS)
    def _(i):
        pltpu.make_async_remote_copy(
            src_ref=wave_me, dst_ref=wave_set.at[a], send_sem=sem_w1.at[0], recv_sem=sem_w1.at[1],
            device_id=(nth_set(i), b), device_id_type=MESH,
        ).start()

    for e in range(2):
        pltpu.make_async_copy(vall.at[pl.ds(0, LEVS - 1)], vall.at[pl.ds(0, LEVS - 1)], sem_v.at[e]).wait()
    for f in range(2):
        vt[f] = vall[:, f].reshape(128, 128).astype(F32).T.astype(BF16)

    def local(p, n):
        src, dst = (
            (xbuf.at[p, a, 0], ra.at[p, a]),
            (ra.at[p, :, y], dbuf.at[p, b]),
            (xbuf.at[p, :, 1, y], rb.at[p, b]),
            (rb.at[p, :, a], dbuf.at[p, :, a]),
        )[n]
        return pltpu.make_async_copy(src, dst, sem_loc.at[n, p])

    def wait_bytes(ref, sem):
        pltpu.make_async_copy(ref, ref, sem).wait()

    def to_lev(p, core_to, src, dst, sems):
        def one(i):
            t = lax.rem(y + i, 4)
            pltpu.make_async_remote_copy(
                src_ref=src(t), dst_ref=dst, send_sem=sems.at[0, p], recv_sem=sems.at[1, p],
                device_id=(a, 2 * t + core_to), device_id_type=MESH,
            ).start()

        @pl.loop(1, 4)
        def _(i):
            one(i)

        @pl.when(core != core_to)
        def _():
            one(0)

    def wait_sent_lev(p, core_to, sems):
        wait_bytes(dbuf.at[p, pl.ds(0, 3)], sems.at[0, p])

        @pl.when(core != core_to)
        def _():
            wait_bytes(dbuf.at[p, 0], sems.at[0, p])

    def send1(p):
        local(p, 0).start()

        @pl.loop(1, SETS)
        def _(i):
            t = nth_set(i)
            pltpu.make_async_remote_copy(
                src_ref=xbuf.at[p, t, 0], dst_ref=ra.at[p, a], send_sem=sem_a1.at[0, p], recv_sem=sem_a1.at[1, p],
                device_id=(t, b), device_id_type=MESH,
            ).start()

        to_lev(p, 1, lambda t: xbuf.at[p, :, 1, t], rb.at[p, b], sem_b1)

        @pl.when(core == 1)
        def _():
            local(p, 2).start()

    def send2(p):
        local(p, 0).wait()
        wait_bytes(ra.at[p, pl.ds(0, SETS - 1)], sem_a1.at[1, p])

        @pl.when(core == 0)
        def _():
            local(p, 1).start()

        to_lev(p, 0, lambda t: ra.at[p, :, t], dbuf.at[p, b], sem_a2)

        @pl.when(core == 1)
        def _():
            local(p, 2).wait()
            wait_bytes(rb.at[p, pl.ds(0, LEVS - 1)], sem_b1.at[1, p])
            local(p, 3).start()

            @pl.loop(1, SETS)
            def _(i):
                t = nth_set(i)
                pltpu.make_async_remote_copy(
                    src_ref=rb.at[p, :, t], dst_ref=dbuf.at[p, :, a],
                    send_sem=sem_b2.at[0, p], recv_sem=sem_b2.at[1, p], device_id=(t, b), device_id_type=MESH,
                ).start()

    def wait2(p):
        @pl.when(core == 0)
        def _():
            local(p, 1).wait()
            wait_bytes(dbuf.at[p, pl.ds(0, LEVS - 1)], sem_a2.at[1, p])

        @pl.when(core == 1)
        def _():
            local(p, 3).wait()
            wait_bytes(dbuf.at[p, :, pl.ds(0, SETS - 1)], sem_b2.at[1, p])

    def waits_of_sends(p):
        wait_bytes(ra.at[p, pl.ds(0, SETS - 1)], sem_a1.at[0, p])
        wait_sent_lev(p, 1, sem_b1)
        wait_sent_lev(p, 0, sem_a2)

        @pl.when(core == 1)
        def _():
            wait_bytes(dbuf.at[p, :, pl.ds(0, SETS - 1)], sem_b2.at[0, p])

    def legendre(p):
        m = wave[p]
        for c in load_spec(p):
            c.wait()
        for f in range(2):
            end = slast[f, p].reshape(2, 128).astype(F32)
            sbuf[f, p, 2560:2576] = jnp.concatenate([end, jnp.zeros((14, 128), F32)], axis=0).astype(BF16)

        @pl.loop(0, PAD // BLK)
        def _(t):
            j0 = pl.multiple_of(t * BLK, BLK)
            j = iota((2 * BLK, 128), 0) // 2 + j0
            degree = jnp.where(j <= TRUNC - m, m + j, j - 1)
            scale = (degree * (degree + 1)).astype(F32) * (1.0 / (TRUNC * (TRUNC + 1)))
            for f in range(2):
                x = sbuf[f, p, pl.ds(pl.multiple_of(2 * t * BLK, 2 * BLK), 2 * BLK), :]
                coupled = jnp.dot(x, vt[f], preferred_element_type=F32)
                adjf[f] = x.astype(F32) + scale * coupled
                for r in range(2):
                    abuf[pl.ds(j0, BLK), (2 * f + r) * 128 : (2 * f + r + 1) * 128] = adjf[
                        f, pl.ds(r, BLK, stride=2), :
                    ].astype(BF16)

        w_low = jnp.where(m == 0, 1.0, 2.0)
        jl = iota((256, HIGH0), 1) + HIGH0
        edge = tpt[p, :, HIGH0:1280].astype(F32)
        low_hi = jnp.where(jl <= TRUNC - m, edge * w_low, 0.0).astype(BF16)
        low = jnp.dot(
            (tpt[p, :, 0:HIGH0].astype(F32) * w_low).astype(BF16), abuf[0:HIGH0, :], preferred_element_type=F32
        )
        low = low + jnp.dot(low_hi, abuf[HIGH0:1280, :], preferred_element_type=F32)
        jh = iota((256, PAD - HIGH0), 1) + HIGH0
        keep = jnp.logical_and(jh > TRUNC - m, jh < ROWS)
        high_t = jnp.where(keep, tpt[p, :, HIGH0:PAD].astype(F32) * 2.0, 0.0).astype(BF16)
        high = jnp.dot(high_t, abuf[HIGH0:PAD, :], preferred_element_type=F32)
        band = jnp.concatenate([low.astype(BF16), high.astype(BF16)], axis=1)
        for q in range(4):
            placed = jnp.dot(band, place[:, q * 256 : q * 256 + 256], preferred_element_type=F32).astype(BF16)
            for e in range(2):
                for s in range(SETS):
                    xbuf[p, s, e, q] = placed[16 * s : 16 * s + 16, 128 * e : 128 * e + 128]

    def pass_waves():
        for e in range(2):
            pltpu.make_async_copy(
                wave_set.at[pl.ds(0, SETS - 1)], wave_set.at[pl.ds(0, SETS - 1)], sem_w1.at[e]
            ).wait()
        wave_set[a] = wave_me[...]
        packed = wave_set[:, 0, :]
        wave_pack[...] = packed
        wave_all[b] = packed

        @pl.loop(1, LEVS)
        def _(i):
            pltpu.make_async_remote_copy(
                src_ref=wave_pack, dst_ref=wave_all.at[b], send_sem=sem_w2.at[0], recv_sem=sem_w2.at[1],
                device_id=(a, nth_lev(i)), device_id_type=MESH,
            ).start()

    @pl.loop(0, PAIRS)
    def _(p):
        legendre(p)
        send1(p)

        @pl.when(p == 0)
        def _():
            pass_waves()

        @pl.when(p >= 2)
        def _():
            send2(p - 2)

    for e in range(2):
        pltpu.make_async_copy(
            wave_all.at[pl.ds(0, LEVS - 1)], wave_all.at[pl.ds(0, LEVS - 1)], sem_w2.at[e]
        ).wait()

    wave_t[...] = wave_all[...].reshape(128, 128).T

    def tables(p):
        waves = wave_all[...].reshape(128, 128)
        mine = jnp.sum(jnp.where(iota((128, 128), 1) == p, waves, 0.0), axis=1, keepdims=True)
        m_all = jnp.broadcast_to(mine, (128, 128))
        wcol[...] = m_all
        sc, sn = turn(m_all * 128.0, clane[0:1, :], clane[1:2, :])
        m_row = jnp.broadcast_to(wave_t[pl.ds(p, 1), :], (8, 128))
        shift_c, shift_s = turn(m_row * SPAN, cval[...], cinv[...])
        shift[p, 0] = shift_c
        shift[p, 1] = shift_s
        step[0] = sc
        step[1] = sn

        @pl.loop(0, SLOTS)
        def _(s):
            count = cval[pl.ds(s, 1), :]
            inverse = cinv[pl.ds(s, 1), :]
            row = pl.multiple_of(p * 256, 256)
            pick_s = iota((32, 128), 1) == s
            for g in range(4):
                rows = slice(32 * g, 32 * g + 32)
                c, n = turn(wcol[rows, :] * iota((32, 128), 1).astype(F32), count, inverse)
                sc, sn = (
                    jnp.broadcast_to(
                        jnp.sum(jnp.where(pick_s, step[e, rows, :], 0.0), axis=1, keepdims=True), (32, 128)
                    )
                    for e in range(2)
                )
                for t in range(SPAN // 128):
                    table[s, pl.ds(row + 32 * g, 32), 128 * t : 128 * t + 128] = c.astype(BF16)
                    table[s, pl.ds(row + 128 + 32 * g, 32), 128 * t : 128 * t + 128] = n.astype(BF16)
                    if t < SPAN // 128 - 1:
                        c, n = c * sc - n * sn, n * sc + c * sn

    def gather(p):
        wait2(p)
        df[...] = dbuf[p].reshape(2048, 128).astype(F32)

        @pl.loop(0, SLOTS)
        def _(s):
            tc = shift[p, 0, pl.ds(s, 1), :]
            ts = shift[p, 1, pl.ds(s, 1), :]
            c0 = pl.multiple_of(p * 256, 256)
            c1 = pl.multiple_of(c0 + 128, 128)
            for k in range(2):
                x = df[pl.ds(k * 8 + s, 128, stride=16), :].T
                re0, im0, re1, im1 = x[0:32], x[32:64], x[64:96], x[96:128]
                for t in range(2):
                    if t == 1:
                        re0, im0 = re0 * tc - im0 * ts, re0 * ts + im0 * tc
                        re1, im1 = re1 * tc + im1 * ts, im1 * tc - re1 * ts
                    for g, (v, w) in enumerate(((re0, -im0), (re1, im1), (-im1, re1))):
                        row = 192 * t + 64 * g + 32 * k
                        lhs[s, row : row + 32, pl.ds(c0, 128)] = v.astype(BF16)
                        lhs[s, row : row + 32, pl.ds(c1, 128)] = w.astype(BF16)

    FIRST = 256 * (PAIRS - 1)

    @pl.loop(0, PAIRS)
    def _(p):
        tables(p)

        @pl.when(p < 2)
        def _():
            send2(p + 3)

        @pl.when(p >= 2)
        def _():
            gather(p - 2)

    gather(3)

    @pl.loop(0, SLOTS)
    def _(s):
        for t in range(SPAN // 256):
            cols = slice(256 * t, 256 * t + 256)
            acc[s, :, cols] = jnp.dot(lhs[s, :, 0:FIRST], table[s, 0:FIRST, cols], preferred_element_type=F32)

    gather(4)

    @pl.loop(0, SLOTS)
    def _(s):
        count = jnp.concatenate([cval[pl.ds(s, 1), :]] * 2, axis=1)
        for t in range(SPAN // 256):
            cols = slice(256 * t, 256 * t + 256)
            total = acc[s, :, cols] + jnp.dot(
                lhs[s, :, FIRST : 256 * PAIRS], table[s, FIRST : 256 * PAIRS, cols], preferred_element_type=F32
            )
            for u in range(2):
                first = SPAN * u + 256 * t
                pc = psi_c[pl.ds(s, 1), first : first + 256]
                ps = psi_s[pl.ds(s, 1), first : first + 256]
                r = 192 * u
                o = total[r : r + 64] + pc * total[r + 64 : r + 128] + ps * total[r + 128 : r + 192]
                lon = (iota((64, 256), 1) + first).astype(F32)
                o = jnp.where(lon < count, o, 0.0)
                for e in range(2):
                    outf[first // 128 + e, pl.ds(s, 64, stride=8), :] = o[:, 128 * e : 128 * e + 128]

    for t in range(8):
        outb[:, :, :, :, 128 * t : 128 * t + 128] = outf[t].reshape(2, 2, 16, 8, 128).astype(BF16)
    done = [
        pltpu.make_async_copy(outb.at[0], out_f, sem_out.at[0]),
        pltpu.make_async_copy(outb.at[1], out_s, sem_out.at[1]),
    ]
    for c in done:
        c.start()

    @pl.loop(0, PAIRS)
    def _(p):
        waits_of_sends(p)

    for c in done:
        c.wait()


def body(spectral, vertical, value_table, slope_table, wave_low, lat_slot, lon_counts):
    rows_first = jnp.transpose(spectral, (0, 3, 4, 2, 1))
    anywhere = pl.BlockSpec(memory_space=pl.ANY)
    scalars = pl.BlockSpec(memory_space=pltpu.SMEM)
    dma = pltpu.SemaphoreType.DMA
    out = jax.ShapeDtypeStruct((2, 16, SLOTS, LONS), BF16)
    return pl.pallas_call(
        kernel,
        out_shape=(out, out),
        in_specs=[anywhere] * 4 + [scalars] * 3 + [pl.BlockSpec(memory_space=pltpu.VMEM)],
        out_specs=(anywhere, anywhere),
        scratch_shapes=[
            pltpu.VMEM((2, PAIRS, 2 * PAD, 128), BF16),
            pltpu.VMEM((2, PAIRS, 1, 2, 128), BF16),
            pltpu.VMEM((2, PAIRS, ROWS, 128), BF16),
            pltpu.VMEM((PAIRS, 256, PAD), BF16),
            pltpu.VMEM((1024, 1024), BF16),
            pltpu.VMEM((PAD, 512), BF16),
            pltpu.VMEM((2, 2 * BLK, 128), F32),
            pltpu.VMEM((PAIRS, SETS, 2, 4, 16, 128), BF16),
            pltpu.VMEM((PAIRS, SETS, 4, 16, 128), BF16),
            pltpu.VMEM((PAIRS, LEVS, SETS, 16, 128), BF16),
            pltpu.VMEM((PAIRS, LEVS, SETS, 16, 128), BF16),
            pltpu.VMEM((LEVS, 2, 16, 128), BF16),
            pltpu.VMEM((2, 128, 128), BF16),
            pltpu.VMEM((8, 128), F32),
            pltpu.VMEM((SETS, 8, 128), F32),
            pltpu.VMEM((SETS, 128), F32),
            pltpu.VMEM((LEVS, SETS, 128), F32),
            pltpu.VMEM((128, 128), F32),
            pltpu.VMEM((128, 128), F32),
            pltpu.VMEM((PAIRS, 2, 8, 128), F32),
            pltpu.VMEM((2, 128, 128), F32),
            pltpu.VMEM((8, 128), F32),
            pltpu.VMEM((8, 128), F32),
            pltpu.VMEM((8, 128), F32),
            pltpu.VMEM((8, LONS), F32),
            pltpu.VMEM((8, LONS), F32),
            pltpu.VMEM((SLOTS, PAIRS * 256, SPAN), BF16),
            pltpu.VMEM((SLOTS, 384, PAIRS * 256), BF16),
            pltpu.VMEM((SLOTS, 384, SPAN), F32),
            pltpu.VMEM((2048, 128), F32),
            pltpu.VMEM((8, 512, 128), F32),
            pltpu.VMEM((2, 2, 16, SLOTS, LONS), BF16),
            dma((4, PAIRS)),
            dma((2, PAIRS)),
            dma((3,)),
            dma((2,)),
            dma((2,)),
            dma((2, PAIRS)),
            dma((2, PAIRS)),
            dma((2, PAIRS)),
            dma((2, PAIRS)),
            dma((4, PAIRS)),
            dma((2,)),
        ],
        compiler_params=pltpu.CompilerParams(
            collective_id=0, has_side_effects=True, vmem_limit_bytes=62 * 2**20
        ),
    )(
        rows_first, vertical, value_table, slope_table, wave_low, lat_slot, lon_counts,
        lat_slot.reshape(1, 128),
    )


def solution(mesh):
    placed = (
        P(None, None, None, ("set", "lev"), None),
        P(None, "lev", None),
        P(("set", "lev"), None, None),
        P(("set", "lev"), None, None),
        P(("set", "lev")),
        P(),
        P(),
    )
    return jax.shard_map(
        body,
        mesh=mesh,
        in_specs=placed,
        out_specs=(P(None, "lev", "set", None), P(None, "lev", "set", None)),
        check_vma=False,
    )
```

```python
import functools

import jax
import jax.numpy as jnp
from jax import lax
from jax.experimental import pallas as pl
from jax.experimental.pallas import tpu as pltpu
from jax.sharding import PartitionSpec as P

TRUNC = 1279
ROWS = 1281
PAIRS = 5
SETS = 16
LEVS = 8
SLOTS = 8
LONS = 1024
SPAN = 256
PAD = 1408
BLK = 704
HIGH0 = 640
MESH = pl.DeviceIdType.MESH
F32 = jnp.float32
BF16 = jnp.bfloat16


def iota(shape, dim):
    return lax.broadcasted_iota(jnp.int32, shape, dim)


def turn(x, count, inverse):
    t = x * inverse
    t = (x - jnp.floor(t + 0.5) * count) * inverse
    t2 = t * t
    sn = t * (3.141590284 + t2 * (-5.167407698 + t2 * (2.544020811 + t2 * (-0.559489909))))
    cs = 0.999993295 + t2 * (-4.933938015 + t2 * (4.041283824 + t2 * (-1.222127058)))
    return 1.0 - 2.0 * sn * sn, 2.0 * sn * cs


def kernel(
    spec, vert, tabs_v, tabs_s, wave, lat, counts, lat_row,
    out_f, out_s,
    sbuf, slast, tbuf, tpt, place, abuf, adjf, xbuf, ra, rb, dbuf, vall, vt,
    wave_me, wave_set, wave_pack, wave_all, wcol, wave_t, shift, step, clane, cval, cinv, psi_c, psi_s,
    table, lhs, acc, df, outf, outb,
    sem_s, sem_t, sem_v, sem_w1, sem_w2, sem_a1, sem_b1, sem_a2, sem_b2, sem_loc, sem_out,
):
    a = lax.axis_index("set")
    b = lax.axis_index("lev")
    y, core = b // 2, lax.rem(b, 2)

    def nth_set(i):
        return lax.rem(a + i, SETS)

    def nth_lev(i):
        return lax.rem(b + i, LEVS)

    def load_tables(p):
        return [pltpu.make_async_copy(t.at[p], tbuf.at[e, p], sem_t.at[e, p]) for e, t in enumerate((tabs_v, tabs_s))]

    def load_spec(p):
        return [
            pltpu.make_async_copy(
                spec.at[f, p, pl.ds(0, 1280)].reshape(2560, 128), sbuf.at[f, p, pl.ds(0, 2560)], sem_s.at[f, p]
            )
            for f in range(2)
        ]

    load_ends = pltpu.make_async_copy(spec.at[:, :, pl.ds(1280, 1)], slast, sem_s.at[2, 0])
    own_v = pltpu.make_async_copy(vert, vall.at[b], sem_v.at[2])
    own_v.start()

    bar = pltpu.get_barrier_semaphore()

    @pl.loop(1, LEVS)
    def _(i):
        pl.semaphore_signal(bar, inc=1, device_id=(a, nth_lev(i)), device_id_type=MESH)

    @pl.loop(1, SETS)
    def _(i):
        pl.semaphore_signal(bar, inc=1, device_id=(nth_set(i), b), device_id_type=MESH)

    def load(p):
        for c in load_tables(p) + load_spec(p):
            c.start()

    load(0)
    load_ends.start()

    lane = iota((8, 128), 1)
    row_of_waves = jnp.zeros((8, 128), F32)
    for p in range(PAIRS):
        row_of_waves = jnp.where(lane == p, wave[p].astype(F32), row_of_waves)
    wave_me[...] = row_of_waves

    own_v.wait()
    pl.semaphore_wait(bar, LEVS - 1 + SETS - 1)

    @pl.loop(1, LEVS)
    def _(i):
        pltpu.make_async_remote_copy(
            src_ref=vall.at[b], dst_ref=vall.at[b], send_sem=sem_v.at[0], recv_sem=sem_v.at[1],
            device_id=(a, nth_lev(i)), device_id_type=MESH,
        ).start()

    @pl.loop(1, SETS)
    def _(i):
        pltpu.make_async_remote_copy(
            src_ref=wave_me, dst_ref=wave_set.at[a], send_sem=sem_w1.at[0], recv_sem=sem_w1.at[1],
            device_id=(nth_set(i), b), device_id_type=MESH,
        ).start()

    for p in range(1, PAIRS):
        load(p)

    sub = iota((8, 128), 0)
    cv = jnp.zeros((8, 128), F32)
    for s in range(SLOTS):
        c_s = counts[lat[a * SLOTS + s]].astype(F32)
        cv = jnp.where(sub == s, c_s, cv)
    cval[...] = cv
    clane_row = jnp.ones((1, 128), F32)
    for s in range(SLOTS):
        c_s = counts[lat[a * SLOTS + s]].astype(F32)
        clane_row = jnp.where(iota((1, 128), 1) == s, c_s, clane_row)
    clane[0:1, :] = clane_row
    clane[1:2, :] = 1.0 / clane_row
    cinv[...] = 1.0 / cv
    for t in range(SPAN // 128):
        x = ((iota((8, 128), 1) + t * 128) * TRUNC).astype(F32)
        pc, ps = turn(x, cval[...], cinv[...])
        psi_c[t] = pc
        psi_s[t] = ps

    @pl.loop(0, 8)
    def _(i):
        row = iota((128, 1024), 0)
        col = iota((128, 1024), 1)
        h, f, r = i // 4, (i // 2) % 2, i % 2
        want = (row // 16) * 128 + h * 64 + r * 32 + f * 16 + row % 16
        place[pl.ds(pl.multiple_of(i * 128, 128), 128), :] = jnp.where(col == want, 1.0, 0.0).astype(BF16)

    r_row = iota((256, 128), 0)
    pick = jnp.where(iota((256, 128), 1) == (r_row // 16) * 8 + r_row % 8, 1.0, 0.0).astype(BF16)
    lat_b = jnp.broadcast_to(lat_row[...], (128, 128)).astype(F32).astype(BF16)
    lat_col = lax.dot_general(pick, lat_b, (((1,), (1,)), ((), ())), preferred_element_type=F32)
    hit = lat_col == iota((256, 128), 1).astype(F32)
    k_row = (r_row // 8) % 2
    order = jnp.concatenate(
        [
            jnp.where(jnp.logical_and(hit, k_row == 0), 1.0, 0.0),
            jnp.where(jnp.logical_and(hit, k_row == 1), 1.0, 0.0),
        ],
        axis=1,
    ).astype(BF16)

    for f in range(2):
        for p in range(PAIRS):
            sbuf[f, p, 2576 : 2 * PAD] = jnp.zeros((2 * PAD - 2576, 128), BF16)

    def turn_tables(p):
        for c in load_tables(p):
            c.wait()

        for t in range(5):
            j0 = 256 * t
            both = jnp.concatenate([tbuf[0, p, j0 : j0 + 256], tbuf[1, p, j0 : j0 + 256]], axis=1)
            turned = lax.dot_general(order, both, (((1,), (1,)), ((), ())), preferred_element_type=F32)
            tpt[:, j0 : j0 + 256] = turned.astype(BF16)

        last = jnp.concatenate([tbuf[0, p, 1280:1281], tbuf[1, p, 1280:1281]], axis=1).astype(F32)
        last = jnp.broadcast_to(last, (128, 256))
        last = jnp.where(iota((128, 256), 0) == 0, last, 0.0).astype(BF16)
        turned = lax.dot_general(order, last, (((1,), (1,)), ((), ())), preferred_element_type=F32)
        tpt[:, 1280:PAD] = turned.astype(BF16)

    turn_tables(0)
    for e in range(2):
        pltpu.make_async_copy(vall.at[pl.ds(0, LEVS - 1)], vall.at[pl.ds(0, LEVS - 1)], sem_v.at[e]).wait()
    for f in range(2):
        vt[f] = vall[:, f].reshape(128, 128).astype(F32).T.astype(BF16)

    def local(p, n):
        src, dst = (
            (xbuf.at[p, a, 0], ra.at[p, a]),
            (ra.at[p, :, y], dbuf.at[p, b]),
            (xbuf.at[p, :, 1, y], rb.at[p, b]),
            (rb.at[p, :, a], dbuf.at[p, :, a]),
        )[n]
        return pltpu.make_async_copy(src, dst, sem_loc.at[n, p])

    def wait_bytes(ref, sem):
        pltpu.make_async_copy(ref, ref, sem).wait()

    def to_lev(p, core_to, src, dst, sems):
        def one(i):
            t = lax.rem(y + i, 4)
            pltpu.make_async_remote_copy(
                src_ref=src(t), dst_ref=dst, send_sem=sems.at[0, p], recv_sem=sems.at[1, p],
                device_id=(a, 2 * t + core_to), device_id_type=MESH,
            ).start()

        @pl.loop(1, 4)
        def _(i):
            one(i)

        @pl.when(core != core_to)
        def _():
            one(0)

    def wait_sent_lev(p, core_to, sems):
        wait_bytes(dbuf.at[p, pl.ds(0, 3)], sems.at[0, p])

        @pl.when(core != core_to)
        def _():
            wait_bytes(dbuf.at[p, 0], sems.at[0, p])

    def send1(p):
        local(p, 0).start()

        for i in range(1, SETS):
            t = nth_set(i)
            pltpu.make_async_remote_copy(
                src_ref=xbuf.at[p, t, 0], dst_ref=ra.at[p, a], send_sem=sem_a1.at[0, p], recv_sem=sem_a1.at[1, p],
                device_id=(t, b), device_id_type=MESH,
            ).start()

        to_lev(p, 1, lambda t: xbuf.at[p, :, 1, t], rb.at[p, b], sem_b1)

        @pl.when(core == 1)
        def _():
            local(p, 2).start()

    def send2(p):
        local(p, 0).wait()
        wait_bytes(ra.at[p, pl.ds(0, SETS - 1)], sem_a1.at[1, p])

        @pl.when(core == 0)
        def _():
            local(p, 1).start()

        to_lev(p, 0, lambda t: ra.at[p, :, t], dbuf.at[p, b], sem_a2)

        @pl.when(core == 1)
        def _():
            local(p, 2).wait()
            wait_bytes(rb.at[p, pl.ds(0, LEVS - 1)], sem_b1.at[1, p])
            local(p, 3).start()

            for i in range(1, SETS):
                t = nth_set(i)
                pltpu.make_async_remote_copy(
                    src_ref=rb.at[p, :, t], dst_ref=dbuf.at[p, :, a],
                    send_sem=sem_b2.at[0, p], recv_sem=sem_b2.at[1, p], device_id=(t, b), device_id_type=MESH,
                ).start()

    def wait2(p):
        @pl.when(core == 0)
        def _():
            local(p, 1).wait()
            wait_bytes(dbuf.at[p, pl.ds(0, LEVS - 1)], sem_a2.at[1, p])

        @pl.when(core == 1)
        def _():
            local(p, 3).wait()
            wait_bytes(dbuf.at[p, :, pl.ds(0, SETS - 1)], sem_b2.at[1, p])

    def waits_of_sends(p):
        wait_bytes(ra.at[p, pl.ds(0, SETS - 1)], sem_a1.at[0, p])
        wait_sent_lev(p, 1, sem_b1)
        wait_sent_lev(p, 0, sem_a2)

        @pl.when(core == 1)
        def _():
            wait_bytes(dbuf.at[p, :, pl.ds(0, SETS - 1)], sem_b2.at[0, p])

    def legendre(p):
        m = wave[p]
        for c in load_spec(p):
            c.wait()
        @pl.when(p == 0)
        def _():
            load_ends.wait()

        for f in range(2):
            end = slast[f, p].reshape(2, 128).astype(F32)
            sbuf[f, p, 2560:2576] = jnp.concatenate([end, jnp.zeros((14, 128), F32)], axis=0).astype(BF16)

        @pl.loop(0, PAD // BLK)
        def _(t):
            j0 = pl.multiple_of(t * BLK, BLK)
            j = iota((2 * BLK, 128), 0) // 2 + j0
            degree = jnp.where(j <= TRUNC - m, m + j, j - 1)
            scale = (degree * (degree + 1)).astype(F32) * (1.0 / (TRUNC * (TRUNC + 1)))
            for f in range(2):
                x = sbuf[f, p, pl.ds(pl.multiple_of(2 * t * BLK, 2 * BLK), 2 * BLK), :]
                coupled = jnp.dot(x, vt[f], preferred_element_type=F32)
                adjf[f] = x.astype(F32) + scale * coupled
                for r in range(2):
                    abuf[pl.ds(j0, BLK), (2 * f + r) * 128 : (2 * f + r + 1) * 128] = adjf[
                        f, pl.ds(r, BLK, stride=2), :
                    ].astype(BF16)

        w_low = jnp.where(m == 0, 1.0, 2.0)
        jl = iota((256, HIGH0), 1) + HIGH0
        edge = tpt[:, HIGH0:1280].astype(F32)
        low_hi = jnp.where(jl <= TRUNC - m, edge * w_low, 0.0).astype(BF16)
        low = jnp.dot(
            (tpt[:, 0:HIGH0].astype(F32) * w_low).astype(BF16), abuf[0:HIGH0, :], preferred_element_type=F32
        )
        low = low + jnp.dot(low_hi, abuf[HIGH0:1280, :], preferred_element_type=F32)
        jh = iota((256, PAD - HIGH0), 1) + HIGH0
        keep = jnp.logical_and(jh > TRUNC - m, jh < ROWS)
        high_t = jnp.where(keep, tpt[:, HIGH0:PAD].astype(F32) * 2.0, 0.0).astype(BF16)
        high = jnp.dot(high_t, abuf[HIGH0:PAD, :], preferred_element_type=F32)
        band = jnp.concatenate([low.astype(BF16), high.astype(BF16)], axis=1)
        for q in range(4):
            placed = jnp.dot(band, place[:, q * 256 : q * 256 + 256], preferred_element_type=F32).astype(BF16)
            for e in range(2):
                for s in range(SETS):
                    xbuf[p, s, e, q] = placed[16 * s : 16 * s + 16, 128 * e : 128 * e + 128]

    def pass_waves():
        for e in range(2):
            pltpu.make_async_copy(
                wave_set.at[pl.ds(0, SETS - 1)], wave_set.at[pl.ds(0, SETS - 1)], sem_w1.at[e]
            ).wait()
        wave_set[a] = wave_me[...]
        packed = wave_set[:, 0, :]
        wave_pack[...] = packed
        wave_all[b] = packed

        @pl.loop(1, LEVS)
        def _(i):
            pltpu.make_async_remote_copy(
                src_ref=wave_pack, dst_ref=wave_all.at[b], send_sem=sem_w2.at[0], recv_sem=sem_w2.at[1],
                device_id=(a, nth_lev(i)), device_id_type=MESH,
            ).start()

    @pl.loop(0, PAIRS)
    def _(p):
        legendre(p)
        send1(p)

        @pl.when(p < PAIRS - 1)
        def _():
            turn_tables(p + 1)

        @pl.when(p == 1)
        def _():
            pass_waves()

        @pl.when(p >= 2)
        def _():
            send2(p - 2)

    for e in range(2):
        pltpu.make_async_copy(
            wave_all.at[pl.ds(0, LEVS - 1)], wave_all.at[pl.ds(0, LEVS - 1)], sem_w2.at[e]
        ).wait()

    wave_t[...] = wave_all[...].reshape(128, 128).T

    def tables(p):
        waves = wave_all[...].reshape(128, 128)
        mine = jnp.sum(jnp.where(iota((128, 128), 1) == p, waves, 0.0), axis=1, keepdims=True)
        m_all = jnp.broadcast_to(mine, (128, 128))
        wcol[...] = m_all
        sc, sn = turn(m_all * 128.0, clane[0:1, :], clane[1:2, :])
        m_row = jnp.broadcast_to(wave_t[pl.ds(p, 1), :], (8, 128))
        for h, waves_h in enumerate((m_row, TRUNC - m_row)):
            for t in range(1, LONS // SPAN):
                shift_c, shift_s = turn(waves_h * (SPAN * t), cval[...], cinv[...])
                shift[p, h, t, 0] = shift_c
                shift[p, h, t, 1] = shift_s
        step[0] = sc
        step[1] = sn

        @pl.loop(0, SLOTS)
        def _(s):
            count = cval[pl.ds(s, 1), :]
            inverse = cinv[pl.ds(s, 1), :]
            row = pl.multiple_of(p * 512, 512)
            pick_s = iota((32, 128), 1) == s
            for g in range(4):
                rows = slice(32 * g, 32 * g + 32)
                c, n = turn(wcol[rows, :] * iota((32, 128), 1).astype(F32), count, inverse)
                sc, sn = (
                    jnp.broadcast_to(
                        jnp.sum(jnp.where(pick_s, step[e, rows, :], 0.0), axis=1, keepdims=True), (32, 128)
                    )
                    for e in range(2)
                )
                for t in range(SPAN // 128):
                    cols = slice(128 * t, 128 * t + 128)
                    pc = psi_c[t, pl.ds(s, 1), :]
                    ps = psi_s[t, pl.ds(s, 1), :]
                    for e, v in enumerate((c, n, pc * c + ps * n, ps * c - pc * n)):
                        table[s, pl.ds(row + 128 * e + 32 * g, 32), cols] = v.astype(BF16)
                    if t < SPAN // 128 - 1:
                        c, n = c * sc - n * sn, n * sc + c * sn

    def gather(p):
        wait2(p)
        df[...] = dbuf[p].reshape(2048, 128).astype(F32)

        @pl.loop(0, SLOTS)
        def _(s):
            c0 = pl.multiple_of(p * 512, 512)
            for k in range(2):
                x = df[pl.ds(k * 8 + s, 128, stride=16), :].T
                for t in range(LONS // SPAN):
                    for h in range(2):
                        re, im = x[64 * h : 64 * h + 32], x[64 * h + 32 : 64 * h + 64]
                        if t > 0:
                            tc = shift[p, h, t, 0, pl.ds(s, 1), :]
                            ts = shift[p, h, t, 1, pl.ds(s, 1), :]
                            re, im = re * tc - im * ts, re * ts + im * tc
                        row = 64 * t + 32 * k
                        for e, v in enumerate((re, -im)):
                            at = pl.multiple_of(c0 + 256 * h + 128 * e, 128)
                            lhs[s, row : row + 32, pl.ds(at, 128)] = v.astype(BF16)

    FIRST = 512 * (PAIRS - 1)

    @pl.loop(0, PAIRS)
    def _(p):
        tables(p)

        @pl.when(p < 2)
        def _():
            send2(p + 3)

        @pl.when(p >= 2)
        def _():
            gather(p - 2)

    gather(3)

    @pl.loop(0, SLOTS)
    def _(s):
        acc[s] = jnp.dot(lhs[s, :, 0:FIRST], table[s, 0:FIRST, :], preferred_element_type=F32)

    gather(4)

    @pl.loop(0, SLOTS)
    def _(s):
        count = jnp.concatenate([cval[pl.ds(s, 1), :]] * 2, axis=1)
        total = acc[s] + jnp.dot(
            lhs[s, :, FIRST : 512 * PAIRS], table[s, FIRST : 512 * PAIRS, :], preferred_element_type=F32
        )
        for t in range(LONS // SPAN):
            lon = (iota((64, 256), 1) + SPAN * t).astype(F32)
            o = jnp.where(lon < count, total[64 * t : 64 * t + 64], 0.0)
            for e in range(2):
                outf[2 * t + e, pl.ds(s, 64, stride=8), :] = o[:, 128 * e : 128 * e + 128]

    for t in range(8):
        outb[:, :, :, :, 128 * t : 128 * t + 128] = outf[t].reshape(2, 2, 16, 8, 128).astype(BF16)
    done = [
        pltpu.make_async_copy(outb.at[0], out_f, sem_out.at[0]),
        pltpu.make_async_copy(outb.at[1], out_s, sem_out.at[1]),
    ]
    for c in done:
        c.start()

    @pl.loop(0, PAIRS)
    def _(p):
        waits_of_sends(p)

    for c in done:
        c.wait()


def hand_over(in_f, in_s, out_f, out_s, held, sems):
    parts = [(n, f, h) for n in range(2) for f in range(2) for h in range(2)]

    def come(n, f, h):
        src = (in_f, in_s)[n].at[f, pl.ds(8 * h, 8)]
        return pltpu.make_async_copy(src, held.at[n, f, pl.ds(8 * h, 8)], sems.at[0, n, f, h])

    def go(n, f, h):
        dst = (out_f, out_s)[n].at[f, pl.ds(8 * h, 8)]
        return pltpu.make_async_copy(held.at[n, f, pl.ds(8 * h, 8)], dst, sems.at[1, n, f, h])

    for part in parts:
        come(*part).start()
    for part in parts:
        come(*part).wait()
        go(*part).start()
    for part in parts:
        go(*part).wait()


def body(spectral, vertical, value_table, slope_table, wave_low, lat_slot, lon_counts):
    rows_first = jnp.transpose(spectral, (0, 3, 4, 2, 1))
    anywhere = pl.BlockSpec(memory_space=pl.ANY)
    scalars = pl.BlockSpec(memory_space=pltpu.SMEM)
    dma = pltpu.SemaphoreType.DMA
    out = jax.ShapeDtypeStruct((2, 16, SLOTS, LONS), BF16)
    gridded = pl.pallas_call(
        kernel,
        out_shape=(out, out),
        in_specs=[anywhere] * 4 + [scalars] * 3 + [pl.BlockSpec(memory_space=pltpu.VMEM)],
        out_specs=(anywhere, anywhere),
        scratch_shapes=[
            pltpu.VMEM((2, PAIRS, 2 * PAD, 128), BF16),
            pltpu.VMEM((2, PAIRS, 1, 2, 128), BF16),
            pltpu.VMEM((2, PAIRS, ROWS, 128), BF16),
            pltpu.VMEM((256, PAD), BF16),
            pltpu.VMEM((1024, 1024), BF16),
            pltpu.VMEM((PAD, 512), BF16),
            pltpu.VMEM((2, 2 * BLK, 128), F32),
            pltpu.VMEM((PAIRS, SETS, 2, 4, 16, 128), BF16),
            pltpu.VMEM((PAIRS, SETS, 4, 16, 128), BF16),
            pltpu.VMEM((PAIRS, LEVS, SETS, 16, 128), BF16),
            pltpu.VMEM((PAIRS, LEVS, SETS, 16, 128), BF16),
            pltpu.VMEM((LEVS, 2, 16, 128), BF16),
            pltpu.VMEM((2, 128, 128), BF16),
            pltpu.VMEM((8, 128), F32),
            pltpu.VMEM((SETS, 8, 128), F32),
            pltpu.VMEM((SETS, 128), F32),
            pltpu.VMEM((LEVS, SETS, 128), F32),
            pltpu.VMEM((128, 128), F32),
            pltpu.VMEM((128, 128), F32),
            pltpu.VMEM((PAIRS, 2, LONS // SPAN, 2, 8, 128), F32),
            pltpu.VMEM((2, 128, 128), F32),
            pltpu.VMEM((8, 128), F32),
            pltpu.VMEM((8, 128), F32),
            pltpu.VMEM((8, 128), F32),
            pltpu.VMEM((SPAN // 128, 8, 128), F32),
            pltpu.VMEM((SPAN // 128, 8, 128), F32),
            pltpu.VMEM((SLOTS, PAIRS * 512, SPAN), BF16),
            pltpu.VMEM((SLOTS, 256, PAIRS * 512), BF16),
            pltpu.VMEM((SLOTS, 256, SPAN), F32),
            pltpu.VMEM((2048, 128), F32),
            pltpu.VMEM((8, 512, 128), F32),
            pltpu.VMEM((2, 2, 16, SLOTS, LONS), BF16),
            dma((3, PAIRS)),
            dma((2, PAIRS)),
            dma((3,)),
            dma((2,)),
            dma((2,)),
            dma((2, PAIRS)),
            dma((2, PAIRS)),
            dma((2, PAIRS)),
            dma((2, PAIRS)),
            dma((4, PAIRS)),
            dma((2,)),
        ],
        compiler_params=pltpu.CompilerParams(
            collective_id=0, has_side_effects=True, vmem_limit_bytes=62 * 2**20
        ),
    )(
        rows_first, vertical, value_table, slope_table, wave_low, lat_slot, lon_counts,
        lat_slot.reshape(1, 128),
    )
    return pl.pallas_call(
        hand_over,
        out_shape=(out, out),
        in_specs=[anywhere] * 2,
        out_specs=(anywhere, anywhere),
        scratch_shapes=[pltpu.VMEM((2, 2, 16, SLOTS, LONS), BF16), dma((2, 2, 2, 2))],
    )(*gridded)


def solution(mesh):
    placed = (
        P(None, None, None, ("set", "lev"), None),
        P(None, "lev", None),
        P(("set", "lev"), None, None),
        P(("set", "lev"), None, None),
        P(("set", "lev")),
        P(),
        P(),
    )
    return jax.shard_map(
        body,
        mesh=mesh,
        in_specs=placed,
        out_specs=(P(None, "lev", "set", None), P(None, "lev", "set", None)),
        check_vma=False,
    )
```

```python
import functools

import jax
import jax.numpy as jnp
from jax import lax
from jax.experimental import pallas as pl
from jax.experimental.pallas import tpu as pltpu
from jax.sharding import PartitionSpec as P

TRUNC = 1279
ROWS = 1281
PAIRS = 5
SETS = 16
LEVS = 8
SLOTS = 8
LONS = 1024
SPAN = 256
PAD = 1408
BLK = 704
HIGH0 = 640
MESH = pl.DeviceIdType.MESH
F32 = jnp.float32
BF16 = jnp.bfloat16


def iota(shape, dim):
    return lax.broadcasted_iota(jnp.int32, shape, dim)


def turn(x, count, inverse):
    t = x * inverse
    t = (x - jnp.floor(t + 0.5) * count) * inverse
    t2 = t * t
    sn = t * (3.141590284 + t2 * (-5.167407698 + t2 * (2.544020811 + t2 * (-0.559489909))))
    cs = 0.999993295 + t2 * (-4.933938015 + t2 * (4.041283824 + t2 * (-1.222127058)))
    return 1.0 - 2.0 * sn * sn, 2.0 * sn * cs


def kernel(
    spec, vert, tabs_v, tabs_s, wave, lat, counts, lat_row,
    out_f, out_s,
    sbuf, slast, tbuf, tpt, place, abuf, adjf, xbuf, ra, rb, dbuf, vall, vt,
    wave_me, wave_set, wave_pack, wave_all, wcol, wave_t, shift, step, clane, cval, cinv, psi_c, psi_s,
    table, lhs, acc, df, outf, outb,
    sem_s, sem_t, sem_v, sem_w1, sem_w2, sem_a1, sem_b1, sem_a2, sem_b2, sem_loc, sem_out,
):
    a = lax.axis_index("set")
    b = lax.axis_index("lev")
    y, core = b // 2, lax.rem(b, 2)

    def nth_set(i):
        return lax.rem(a + i, SETS)

    def nth_lev(i):
        return lax.rem(b + i, LEVS)

    def load_tables(p):
        return [pltpu.make_async_copy(t.at[p], tbuf.at[e, p], sem_t.at[e, p]) for e, t in enumerate((tabs_v, tabs_s))]

    def load_spec(p):
        return [
            pltpu.make_async_copy(
                spec.at[f, p, pl.ds(0, 1280)].reshape(2560, 128), sbuf.at[f, p, pl.ds(0, 2560)], sem_s.at[f, p]
            )
            for f in range(2)
        ]

    load_ends = pltpu.make_async_copy(spec.at[:, :, pl.ds(1280, 1)], slast, sem_s.at[2, 0])
    own_v = pltpu.make_async_copy(vert, vall.at[b], sem_v.at[2])
    own_v.start()

    bar = pltpu.get_barrier_semaphore()

    @pl.loop(1, LEVS)
    def _(i):
        pl.semaphore_signal(bar, inc=1, device_id=(a, nth_lev(i)), device_id_type=MESH)

    @pl.loop(1, SETS)
    def _(i):
        pl.semaphore_signal(bar, inc=1, device_id=(nth_set(i), b), device_id_type=MESH)

    def load(p):
        for c in load_tables(p) + load_spec(p):
            c.start()

    load(0)
    load_ends.start()

    lane = iota((8, 128), 1)
    row_of_waves = jnp.zeros((8, 128), F32)
    for p in range(PAIRS):
        row_of_waves = jnp.where(lane == p, wave[p].astype(F32), row_of_waves)
    wave_me[...] = row_of_waves

    own_v.wait()
    pl.semaphore_wait(bar, LEVS - 1 + SETS - 1)

    @pl.loop(1, LEVS)
    def _(i):
        pltpu.make_async_remote_copy(
            src_ref=vall.at[b], dst_ref=vall.at[b], send_sem=sem_v.at[0], recv_sem=sem_v.at[1],
            device_id=(a, nth_lev(i)), device_id_type=MESH,
        ).start()

    @pl.loop(1, SETS)
    def _(i):
        pltpu.make_async_remote_copy(
            src_ref=wave_me, dst_ref=wave_set.at[a], send_sem=sem_w1.at[0], recv_sem=sem_w1.at[1],
            device_id=(nth_set(i), b), device_id_type=MESH,
        ).start()

    for p in range(1, PAIRS):
        load(p)

    sub = iota((8, 128), 0)
    cv = jnp.zeros((8, 128), F32)
    for s in range(SLOTS):
        c_s = counts[lat[a * SLOTS + s]].astype(F32)
        cv = jnp.where(sub == s, c_s, cv)
    cval[...] = cv
    clane_row = jnp.ones((1, 128), F32)
    for s in range(SLOTS):
        c_s = counts[lat[a * SLOTS + s]].astype(F32)
        clane_row = jnp.where(iota((1, 128), 1) == s, c_s, clane_row)
    clane[0:1, :] = clane_row
    clane[1:2, :] = 1.0 / clane_row
    cinv[...] = 1.0 / cv
    for t in range(SPAN // 128):
        x = ((iota((8, 128), 1) + t * 128) * TRUNC).astype(F32)
        pc, ps = turn(x, cval[...], cinv[...])
        psi_c[t] = pc
        psi_s[t] = ps

    @pl.loop(0, 8)
    def _(i):
        row = iota((128, 1024), 0)
        col = iota((128, 1024), 1)
        h, f, r = i // 4, (i // 2) % 2, i % 2
        want = (row // 16) * 128 + h * 64 + r * 32 + f * 16 + row % 16
        place[pl.ds(pl.multiple_of(i * 128, 128), 128), :] = jnp.where(col == want, 1.0, 0.0).astype(BF16)

    r_row = iota((256, 128), 0)
    pick = jnp.where(iota((256, 128), 1) == (r_row // 16) * 8 + r_row % 8, 1.0, 0.0).astype(BF16)
    lat_b = jnp.broadcast_to(lat_row[...], (128, 128)).astype(F32).astype(BF16)
    lat_col = lax.dot_general(pick, lat_b, (((1,), (1,)), ((), ())), preferred_element_type=F32)
    hit = lat_col == iota((256, 128), 1).astype(F32)
    k_row = (r_row // 8) % 2
    order = jnp.concatenate(
        [
            jnp.where(jnp.logical_and(hit, k_row == 0), 1.0, 0.0),
            jnp.where(jnp.logical_and(hit, k_row == 1), 1.0, 0.0),
        ],
        axis=1,
    ).astype(BF16)

    for f in range(2):
        for p in range(PAIRS):
            sbuf[f, p, 2576 : 2 * PAD] = jnp.zeros((2 * PAD - 2576, 128), BF16)

    def turn_tables(p):
        for c in load_tables(p):
            c.wait()

        for t in range(5):
            j0 = 256 * t
            both = jnp.concatenate([tbuf[0, p, j0 : j0 + 256], tbuf[1, p, j0 : j0 + 256]], axis=1)
            turned = lax.dot_general(order, both, (((1,), (1,)), ((), ())), preferred_element_type=F32)
            tpt[:, j0 : j0 + 256] = turned.astype(BF16)

        last = jnp.concatenate([tbuf[0, p, 1280:1281], tbuf[1, p, 1280:1281]], axis=1).astype(F32)
        last = jnp.broadcast_to(last, (128, 256))
        last = jnp.where(iota((128, 256), 0) == 0, last, 0.0).astype(BF16)
        turned = lax.dot_general(order, last, (((1,), (1,)), ((), ())), preferred_element_type=F32)
        tpt[:, 1280:PAD] = turned.astype(BF16)

    turn_tables(0)
    for e in range(2):
        pltpu.make_async_copy(vall.at[pl.ds(0, LEVS - 1)], vall.at[pl.ds(0, LEVS - 1)], sem_v.at[e]).wait()
    for f in range(2):
        vt[f] = vall[:, f].reshape(128, 128).astype(F32).T.astype(BF16)

    def local(p, n):
        src, dst = (
            (xbuf.at[p, a, 0], ra.at[p, a]),
            (ra.at[p, :, y], dbuf.at[p, b]),
            (xbuf.at[p, :, 1, y], rb.at[p, b]),
            (rb.at[p, :, a], dbuf.at[p, :, a]),
        )[n]
        return pltpu.make_async_copy(src, dst, sem_loc.at[n, p])

    def wait_bytes(ref, sem):
        pltpu.make_async_copy(ref, ref, sem).wait()

    def to_lev(p, core_to, src, dst, sems):
        def one(i):
            t = lax.rem(y + i, 4)
            pltpu.make_async_remote_copy(
                src_ref=src(t), dst_ref=dst, send_sem=sems.at[0, p], recv_sem=sems.at[1, p],
                device_id=(a, 2 * t + core_to), device_id_type=MESH,
            ).start()

        @pl.loop(1, 4)
        def _(i):
            one(i)

        @pl.when(core != core_to)
        def _():
            one(0)

    def wait_sent_lev(p, core_to, sems):
        wait_bytes(dbuf.at[p, pl.ds(0, 3)], sems.at[0, p])

        @pl.when(core != core_to)
        def _():
            wait_bytes(dbuf.at[p, 0], sems.at[0, p])

    def send1(p):
        local(p, 0).start()

        for i in range(1, SETS):
            t = nth_set(i)
            pltpu.make_async_remote_copy(
                src_ref=xbuf.at[p, t, 0], dst_ref=ra.at[p, a], send_sem=sem_a1.at[0, p], recv_sem=sem_a1.at[1, p],
                device_id=(t, b), device_id_type=MESH,
            ).start()

        to_lev(p, 1, lambda t: xbuf.at[p, :, 1, t], rb.at[p, b], sem_b1)

        @pl.when(core == 1)
        def _():
            local(p, 2).start()

    def send2(p):
        local(p, 0).wait()
        wait_bytes(ra.at[p, pl.ds(0, SETS - 1)], sem_a1.at[1, p])

        @pl.when(core == 0)
        def _():
            local(p, 1).start()

        to_lev(p, 0, lambda t: ra.at[p, :, t], dbuf.at[p, b], sem_a2)

        @pl.when(core == 1)
        def _():
            local(p, 2).wait()
            wait_bytes(rb.at[p, pl.ds(0, LEVS - 1)], sem_b1.at[1, p])
            local(p, 3).start()

            for i in range(1, SETS):
                t = nth_set(i)
                pltpu.make_async_remote_copy(
                    src_ref=rb.at[p, :, t], dst_ref=dbuf.at[p, :, a],
                    send_sem=sem_b2.at[0, p], recv_sem=sem_b2.at[1, p], device_id=(t, b), device_id_type=MESH,
                ).start()

    def wait2(p):
        @pl.when(core == 0)
        def _():
            local(p, 1).wait()
            wait_bytes(dbuf.at[p, pl.ds(0, LEVS - 1)], sem_a2.at[1, p])

        @pl.when(core == 1)
        def _():
            local(p, 3).wait()
            wait_bytes(dbuf.at[p, :, pl.ds(0, SETS - 1)], sem_b2.at[1, p])

    def waits_of_sends(p):
        wait_bytes(ra.at[p, pl.ds(0, SETS - 1)], sem_a1.at[0, p])
        wait_sent_lev(p, 1, sem_b1)
        wait_sent_lev(p, 0, sem_a2)

        @pl.when(core == 1)
        def _():
            wait_bytes(dbuf.at[p, :, pl.ds(0, SETS - 1)], sem_b2.at[0, p])

    def legendre(p):
        m = wave[p]
        for c in load_spec(p):
            c.wait()
        @pl.when(p == 0)
        def _():
            load_ends.wait()

        for f in range(2):
            end = slast[f, p].reshape(2, 128).astype(F32)
            sbuf[f, p, 2560:2576] = jnp.concatenate([end, jnp.zeros((14, 128), F32)], axis=0).astype(BF16)

        @pl.loop(0, PAD // BLK, unroll=2)
        def _(t):
            j0 = pl.multiple_of(t * BLK, BLK)
            j = iota((2 * BLK, 128), 0) // 2 + j0
            degree = jnp.where(j <= TRUNC - m, m + j, j - 1)
            scale = (degree * (degree + 1)).astype(F32) * (1.0 / (TRUNC * (TRUNC + 1)))
            for f in range(2):
                x = sbuf[f, p, pl.ds(pl.multiple_of(2 * t * BLK, 2 * BLK), 2 * BLK), :]
                coupled = jnp.dot(x, vt[f], preferred_element_type=F32)
                adjf[f] = x.astype(F32) + scale * coupled
                for r in range(2):
                    abuf[pl.ds(j0, BLK), (2 * f + r) * 128 : (2 * f + r + 1) * 128] = adjf[
                        f, pl.ds(r, BLK, stride=2), :
                    ].astype(BF16)

        w_low = jnp.where(m == 0, 1.0, 2.0)
        jl = iota((256, HIGH0), 1) + HIGH0
        edge = tpt[:, HIGH0:1280].astype(F32)
        low_hi = jnp.where(jl <= TRUNC - m, edge * w_low, 0.0).astype(BF16)
        low = jnp.dot(
            (tpt[:, 0:HIGH0].astype(F32) * w_low).astype(BF16), abuf[0:HIGH0, :], preferred_element_type=F32
        )
        low = low + jnp.dot(low_hi, abuf[HIGH0:1280, :], preferred_element_type=F32)
        jh = iota((256, PAD - HIGH0), 1) + HIGH0
        keep = jnp.logical_and(jh > TRUNC - m, jh < ROWS)
        high_t = jnp.where(keep, tpt[:, HIGH0:PAD].astype(F32) * 2.0, 0.0).astype(BF16)
        high = jnp.dot(high_t, abuf[HIGH0:PAD, :], preferred_element_type=F32)
        band = jnp.concatenate([low.astype(BF16), high.astype(BF16)], axis=1)
        for q in range(4):
            placed = jnp.dot(band, place[:, q * 256 : q * 256 + 256], preferred_element_type=F32).astype(BF16)
            for e in range(2):
                for s in range(SETS):
                    xbuf[p, s, e, q] = placed[16 * s : 16 * s + 16, 128 * e : 128 * e + 128]

    def pass_waves():
        for e in range(2):
            pltpu.make_async_copy(
                wave_set.at[pl.ds(0, SETS - 1)], wave_set.at[pl.ds(0, SETS - 1)], sem_w1.at[e]
            ).wait()
        wave_set[a] = wave_me[...]
        packed = wave_set[:, 0, :]
        wave_pack[...] = packed
        wave_all[b] = packed

        @pl.loop(1, LEVS)
        def _(i):
            pltpu.make_async_remote_copy(
                src_ref=wave_pack, dst_ref=wave_all.at[b], send_sem=sem_w2.at[0], recv_sem=sem_w2.at[1],
                device_id=(a, nth_lev(i)), device_id_type=MESH,
            ).start()

    @pl.loop(0, PAIRS)
    def _(p):
        legendre(p)
        send1(p)

        @pl.when(p < PAIRS - 1)
        def _():
            turn_tables(p + 1)

        @pl.when(p == 1)
        def _():
            pass_waves()

        @pl.when(p >= 2)
        def _():
            send2(p - 2)

    for e in range(2):
        pltpu.make_async_copy(
            wave_all.at[pl.ds(0, LEVS - 1)], wave_all.at[pl.ds(0, LEVS - 1)], sem_w2.at[e]
        ).wait()

    wave_t[...] = wave_all[...].reshape(128, 128).T

    def tables(p):
        waves = wave_all[...].reshape(128, 128)
        mine = jnp.sum(jnp.where(iota((128, 128), 1) == p, waves, 0.0), axis=1, keepdims=True)
        m_all = jnp.broadcast_to(mine, (128, 128))
        wcol[...] = m_all
        sc, sn = turn(m_all * 128.0, clane[0:1, :], clane[1:2, :])
        m_row = jnp.broadcast_to(wave_t[pl.ds(p, 1), :], (8, 128))
        for h, waves_h in enumerate((m_row, TRUNC - m_row)):
            for t in range(1, LONS // SPAN):
                shift_c, shift_s = turn(waves_h * (SPAN * t), cval[...], cinv[...])
                shift[p, h, t, 0] = shift_c
                shift[p, h, t, 1] = shift_s
        step[0] = sc
        step[1] = sn

        @pl.loop(0, SLOTS)
        def _(s):
            count = cval[pl.ds(s, 1), :]
            inverse = cinv[pl.ds(s, 1), :]
            row = pl.multiple_of(p * 512, 512)
            pick_s = iota((32, 128), 1) == s
            for g in range(4):
                rows = slice(32 * g, 32 * g + 32)
                c, n = turn(wcol[rows, :] * iota((32, 128), 1).astype(F32), count, inverse)
                sc, sn = (
                    jnp.broadcast_to(
                        jnp.sum(jnp.where(pick_s, step[e, rows, :], 0.0), axis=1, keepdims=True), (32, 128)
                    )
                    for e in range(2)
                )
                for t in range(SPAN // 128):
                    cols = slice(128 * t, 128 * t + 128)
                    pc = psi_c[t, pl.ds(s, 1), :]
                    ps = psi_s[t, pl.ds(s, 1), :]
                    for e, v in enumerate((c, n, pc * c + ps * n, ps * c - pc * n)):
                        table[s, pl.ds(row + 128 * e + 32 * g, 32), cols] = v.astype(BF16)
                    if t < SPAN // 128 - 1:
                        c, n = c * sc - n * sn, n * sc + c * sn

    def gather(p):
        wait2(p)
        df[...] = dbuf[p].reshape(2048, 128).astype(F32)

        @pl.loop(0, SLOTS, unroll=4)
        def _(s):
            c0 = pl.multiple_of(p * 512, 512)
            for k in range(2):
                x = df[pl.ds(k * 8 + s, 128, stride=16), :].T
                for t in range(LONS // SPAN):
                    for h in range(2):
                        re, im = x[64 * h : 64 * h + 32], x[64 * h + 32 : 64 * h + 64]
                        if t > 0:
                            tc = shift[p, h, t, 0, pl.ds(s, 1), :]
                            ts = shift[p, h, t, 1, pl.ds(s, 1), :]
                            re, im = re * tc - im * ts, re * ts + im * tc
                        row = 64 * t + 32 * k
                        for e, v in enumerate((re, -im)):
                            at = pl.multiple_of(c0 + 256 * h + 128 * e, 128)
                            lhs[s, row : row + 32, pl.ds(at, 128)] = v.astype(BF16)

    FIRST = 512 * (PAIRS - 1)

    @pl.loop(0, PAIRS)
    def _(p):
        tables(p)

        @pl.when(p < 2)
        def _():
            send2(p + 3)

        @pl.when(p >= 2)
        def _():
            gather(p - 2)

    gather(3)

    @pl.loop(0, SLOTS, unroll=4)
    def _(s):
        acc[s] = jnp.dot(lhs[s, :, 0:FIRST], table[s, 0:FIRST, :], preferred_element_type=F32)

    gather(4)

    @pl.loop(0, SLOTS, unroll=4)
    def _(s):
        count = jnp.concatenate([cval[pl.ds(s, 1), :]] * 2, axis=1)
        total = acc[s] + jnp.dot(
            lhs[s, :, FIRST : 512 * PAIRS], table[s, FIRST : 512 * PAIRS, :], preferred_element_type=F32
        )
        for t in range(LONS // SPAN):
            lon = (iota((64, 256), 1) + SPAN * t).astype(F32)
            o = jnp.where(lon < count, total[64 * t : 64 * t + 64], 0.0)
            for e in range(2):
                outf[2 * t + e, pl.ds(s, 64, stride=8), :] = o[:, 128 * e : 128 * e + 128]

    for t in range(8):
        outb[:, :, :, :, 128 * t : 128 * t + 128] = outf[t].reshape(2, 2, 16, 8, 128).astype(BF16)
    done = [
        pltpu.make_async_copy(outb.at[0], out_f, sem_out.at[0]),
        pltpu.make_async_copy(outb.at[1], out_s, sem_out.at[1]),
    ]
    for c in done:
        c.start()

    @pl.loop(0, PAIRS)
    def _(p):
        waits_of_sends(p)

    for c in done:
        c.wait()


def hand_over(in_f, in_s, out_f, out_s, held, sems):
    parts = [(n, f, h) for n in range(2) for f in range(2) for h in range(2)]

    def come(n, f, h):
        src = (in_f, in_s)[n].at[f, pl.ds(8 * h, 8)]
        return pltpu.make_async_copy(src, held.at[n, f, pl.ds(8 * h, 8)], sems.at[0, n, f, h])

    def go(n, f, h):
        dst = (out_f, out_s)[n].at[f, pl.ds(8 * h, 8)]
        return pltpu.make_async_copy(held.at[n, f, pl.ds(8 * h, 8)], dst, sems.at[1, n, f, h])

    for part in parts:
        come(*part).start()
    for part in parts:
        come(*part).wait()
        go(*part).start()
    for part in parts:
        go(*part).wait()


def body(spectral, vertical, value_table, slope_table, wave_low, lat_slot, lon_counts):
    rows_first = jnp.transpose(spectral, (0, 3, 4, 2, 1))
    anywhere = pl.BlockSpec(memory_space=pl.ANY)
    scalars = pl.BlockSpec(memory_space=pltpu.SMEM)
    dma = pltpu.SemaphoreType.DMA
    out = jax.ShapeDtypeStruct((2, 16, SLOTS, LONS), BF16)
    gridded = pl.pallas_call(
        kernel,
        out_shape=(out, out),
        in_specs=[anywhere] * 4 + [scalars] * 3 + [pl.BlockSpec(memory_space=pltpu.VMEM)],
        out_specs=(anywhere, anywhere),
        scratch_shapes=[
            pltpu.VMEM((2, PAIRS, 2 * PAD, 128), BF16),
            pltpu.VMEM((2, PAIRS, 1, 2, 128), BF16),
            pltpu.VMEM((2, PAIRS, ROWS, 128), BF16),
            pltpu.VMEM((256, PAD), BF16),
            pltpu.VMEM((1024, 1024), BF16),
            pltpu.VMEM((PAD, 512), BF16),
            pltpu.VMEM((2, 2 * BLK, 128), F32),
            pltpu.VMEM((PAIRS, SETS, 2, 4, 16, 128), BF16),
            pltpu.VMEM((PAIRS, SETS, 4, 16, 128), BF16),
            pltpu.VMEM((PAIRS, LEVS, SETS, 16, 128), BF16),
            pltpu.VMEM((PAIRS, LEVS, SETS, 16, 128), BF16),
            pltpu.VMEM((LEVS, 2, 16, 128), BF16),
            pltpu.VMEM((2, 128, 128), BF16),
            pltpu.VMEM((8, 128), F32),
            pltpu.VMEM((SETS, 8, 128), F32),
            pltpu.VMEM((SETS, 128), F32),
            pltpu.VMEM((LEVS, SETS, 128), F32),
            pltpu.VMEM((128, 128), F32),
            pltpu.VMEM((128, 128), F32),
            pltpu.VMEM((PAIRS, 2, LONS // SPAN, 2, 8, 128), F32),
            pltpu.VMEM((2, 128, 128), F32),
            pltpu.VMEM((8, 128), F32),
            pltpu.VMEM((8, 128), F32),
            pltpu.VMEM((8, 128), F32),
            pltpu.VMEM((SPAN // 128, 8, 128), F32),
            pltpu.VMEM((SPAN // 128, 8, 128), F32),
            pltpu.VMEM((SLOTS, PAIRS * 512, SPAN), BF16),
            pltpu.VMEM((SLOTS, 256, PAIRS * 512), BF16),
            pltpu.VMEM((SLOTS, 256, SPAN), F32),
            pltpu.VMEM((2048, 128), F32),
            pltpu.VMEM((8, 512, 128), F32),
            pltpu.VMEM((2, 2, 16, SLOTS, LONS), BF16),
            dma((3, PAIRS)),
            dma((2, PAIRS)),
            dma((3,)),
            dma((2,)),
            dma((2,)),
            dma((2, PAIRS)),
            dma((2, PAIRS)),
            dma((2, PAIRS)),
            dma((2, PAIRS)),
            dma((4, PAIRS)),
            dma((2,)),
        ],
        compiler_params=pltpu.CompilerParams(
            collective_id=0, has_side_effects=True, vmem_limit_bytes=62 * 2**20
        ),
    )(
        rows_first, vertical, value_table, slope_table, wave_low, lat_slot, lon_counts,
        lat_slot.reshape(1, 128),
    )
    return pl.pallas_call(
        hand_over,
        out_shape=(out, out),
        in_specs=[anywhere] * 2,
        out_specs=(anywhere, anywhere),
        scratch_shapes=[pltpu.VMEM((2, 2, 16, SLOTS, LONS), BF16), dma((2, 2, 2, 2))],
    )(*gridded)


def solution(mesh):
    placed = (
        P(None, None, None, ("set", "lev"), None),
        P(None, "lev", None),
        P(("set", "lev"), None, None),
        P(("set", "lev"), None, None),
        P(("set", "lev")),
        P(),
        P(),
    )
    return jax.shard_map(
        body,
        mesh=mesh,
        in_specs=placed,
        out_specs=(P(None, "lev", "set", None), P(None, "lev", "set", None)),
        check_vma=False,
    )
```

```python
import functools

import jax
import jax.numpy as jnp
from jax import lax
from jax.experimental import pallas as pl
from jax.experimental.pallas import tpu as pltpu
from jax.sharding import PartitionSpec as P

TRUNC = 1279
ROWS = 1281
PAIRS = 5
SETS = 16
LEVS = 8
SLOTS = 8
LONS = 1024
SPAN = 256
PAD = 1408
BLK = 704
HIGH0 = 640
MESH = pl.DeviceIdType.MESH
F32 = jnp.float32
BF16 = jnp.bfloat16


def iota(shape, dim):
    return lax.broadcasted_iota(jnp.int32, shape, dim)


def turn(x, count, inverse):
    t = x * inverse
    t = (x - jnp.floor(t + 0.5) * count) * inverse
    t2 = t * t
    sn = t * (3.141590284 + t2 * (-5.167407698 + t2 * (2.544020811 + t2 * (-0.559489909))))
    cs = 0.999993295 + t2 * (-4.933938015 + t2 * (4.041283824 + t2 * (-1.222127058)))
    return 1.0 - 2.0 * sn * sn, 2.0 * sn * cs


def kernel(
    spec, vert, tabs_v, tabs_s, wave, lat, counts, lat_row,
    out_f, out_s,
    sbuf, slast, tbuf, tpt, place, abuf, adjf, xbuf, ra, rb, dbuf, vall, vt,
    wave_me, wave_set, wave_pack, wave_all, wcol, wave_t, shift, step, clane, cval, cinv, psi_c, psi_s,
    table, lhs, acc, df, outf, outb,
    sem_s, sem_t, sem_v, sem_w1, sem_w2, sem_a1, sem_b1, sem_a2, sem_b2, sem_loc, sem_out,
):
    a = lax.axis_index("set")
    b = lax.axis_index("lev")
    y, core = b // 2, lax.rem(b, 2)

    def nth_set(i):
        return lax.rem(a + i, SETS)

    def nth_lev(i):
        return lax.rem(b + i, LEVS)

    def load_tables(p):
        return [pltpu.make_async_copy(t.at[p], tbuf.at[e, p], sem_t.at[e, p]) for e, t in enumerate((tabs_v, tabs_s))]

    def load_spec(p):
        return [
            pltpu.make_async_copy(
                spec.at[f, p, pl.ds(0, 1280)].reshape(2560, 128), sbuf.at[f, p, pl.ds(0, 2560)], sem_s.at[f, p]
            )
            for f in range(2)
        ]

    load_ends = pltpu.make_async_copy(spec.at[:, :, pl.ds(1280, 1)], slast, sem_s.at[2, 0])
    own_v = pltpu.make_async_copy(vert, vall.at[b], sem_v.at[2])
    own_v.start()

    bar = pltpu.get_barrier_semaphore()

    @pl.loop(1, LEVS)
    def _(i):
        pl.semaphore_signal(bar, inc=1, device_id=(a, nth_lev(i)), device_id_type=MESH)

    @pl.loop(1, SETS)
    def _(i):
        pl.semaphore_signal(bar, inc=1, device_id=(nth_set(i), b), device_id_type=MESH)

    def load(p):
        for c in load_tables(p) + load_spec(p):
            c.start()

    load(0)
    load_ends.start()

    lane = iota((8, 128), 1)
    row_of_waves = jnp.zeros((8, 128), F32)
    for p in range(PAIRS):
        row_of_waves = jnp.where(lane == p, wave[p].astype(F32), row_of_waves)
    wave_me[...] = row_of_waves

    own_v.wait()
    pl.semaphore_wait(bar, LEVS - 1 + SETS - 1)

    @pl.loop(1, LEVS)
    def _(i):
        pltpu.make_async_remote_copy(
            src_ref=vall.at[b], dst_ref=vall.at[b], send_sem=sem_v.at[0], recv_sem=sem_v.at[1],
            device_id=(a, nth_lev(i)), device_id_type=MESH,
        ).start()

    @pl.loop(1, SETS)
    def _(i):
        pltpu.make_async_remote_copy(
            src_ref=wave_me, dst_ref=wave_set.at[a], send_sem=sem_w1.at[0], recv_sem=sem_w1.at[1],
            device_id=(nth_set(i), b), device_id_type=MESH,
        ).start()

    for p in range(1, PAIRS):
        load(p)

    sub = iota((8, 128), 0)
    cv = jnp.zeros((8, 128), F32)
    for s in range(SLOTS):
        c_s = counts[lat[a * SLOTS + s]].astype(F32)
        cv = jnp.where(sub == s, c_s, cv)
    cval[...] = cv
    clane_row = jnp.ones((1, 128), F32)
    for s in range(SLOTS):
        c_s = counts[lat[a * SLOTS + s]].astype(F32)
        clane_row = jnp.where(iota((1, 128), 1) == s, c_s, clane_row)
    clane[0:1, :] = clane_row
    clane[1:2, :] = 1.0 / clane_row
    cinv[...] = 1.0 / cv
    for t in range(SPAN // 128):
        x = ((iota((8, 128), 1) + t * 128) * TRUNC).astype(F32)
        pc, ps = turn(x, cval[...], cinv[...])
        psi_c[t] = pc
        psi_s[t] = ps

    @pl.loop(0, 8)
    def _(i):
        row = iota((128, 1024), 0)
        col = iota((128, 1024), 1)
        h, f, r = i // 4, (i // 2) % 2, i % 2
        want = (row // 16) * 128 + h * 64 + r * 32 + f * 16 + row % 16
        place[pl.ds(pl.multiple_of(i * 128, 128), 128), :] = jnp.where(col == want, 1.0, 0.0).astype(BF16)

    r_row = iota((256, 128), 0)
    pick = jnp.where(iota((256, 128), 1) == (r_row // 16) * 8 + r_row % 8, 1.0, 0.0).astype(BF16)
    lat_b = jnp.broadcast_to(lat_row[...], (128, 128)).astype(F32).astype(BF16)
    lat_col = lax.dot_general(pick, lat_b, (((1,), (1,)), ((), ())), preferred_element_type=F32)
    hit = lat_col == iota((256, 128), 1).astype(F32)
    k_row = (r_row // 8) % 2
    order = jnp.concatenate(
        [
            jnp.where(jnp.logical_and(hit, k_row == 0), 1.0, 0.0),
            jnp.where(jnp.logical_and(hit, k_row == 1), 1.0, 0.0),
        ],
        axis=1,
    ).astype(BF16)

    for f in range(2):
        for p in range(PAIRS):
            sbuf[f, p, 2576 : 2 * PAD] = jnp.zeros((2 * PAD - 2576, 128), BF16)

    def turn_tables(p):
        for c in load_tables(p):
            c.wait()

        for t in range(5):
            j0 = 256 * t
            both = jnp.concatenate([tbuf[0, p, j0 : j0 + 256], tbuf[1, p, j0 : j0 + 256]], axis=1)
            turned = lax.dot_general(order, both, (((1,), (1,)), ((), ())), preferred_element_type=F32)
            tpt[:, j0 : j0 + 256] = turned.astype(BF16)

        last = jnp.concatenate([tbuf[0, p, 1280:1281], tbuf[1, p, 1280:1281]], axis=1).astype(F32)
        last = jnp.broadcast_to(last, (128, 256))
        last = jnp.where(iota((128, 256), 0) == 0, last, 0.0).astype(BF16)
        turned = lax.dot_general(order, last, (((1,), (1,)), ((), ())), preferred_element_type=F32)
        tpt[:, 1280:PAD] = turned.astype(BF16)

    turn_tables(0)
    for e in range(2):
        pltpu.make_async_copy(vall.at[pl.ds(0, LEVS - 1)], vall.at[pl.ds(0, LEVS - 1)], sem_v.at[e]).wait()
    for f in range(2):
        vt[f] = vall[:, f].reshape(128, 128).astype(F32).T.astype(BF16)

    def local(p, n):
        src, dst = (
            (xbuf.at[p, a, 0], ra.at[p, a]),
            (ra.at[p, :, y], dbuf.at[p, b]),
            (xbuf.at[p, :, 1, y], rb.at[p, b]),
            (rb.at[p, :, a], dbuf.at[p, :, a]),
        )[n]
        return pltpu.make_async_copy(src, dst, sem_loc.at[n, p])

    def wait_bytes(ref, sem):
        pltpu.make_async_copy(ref, ref, sem).wait()

    def to_lev(p, core_to, src, dst, sems):
        def one(i):
            t = lax.rem(y + i, 4)
            pltpu.make_async_remote_copy(
                src_ref=src(t), dst_ref=dst, send_sem=sems.at[0, p], recv_sem=sems.at[1, p],
                device_id=(a, 2 * t + core_to), device_id_type=MESH,
            ).start()

        @pl.loop(1, 4)
        def _(i):
            one(i)

        @pl.when(core != core_to)
        def _():
            one(0)

    def wait_sent_lev(p, core_to, sems):
        wait_bytes(dbuf.at[p, pl.ds(0, 3)], sems.at[0, p])

        @pl.when(core != core_to)
        def _():
            wait_bytes(dbuf.at[p, 0], sems.at[0, p])

    def send1(p):
        local(p, 0).start()

        for i in range(1, SETS):
            t = nth_set(i)
            pltpu.make_async_remote_copy(
                src_ref=xbuf.at[p, t, 0], dst_ref=ra.at[p, a], send_sem=sem_a1.at[0, p], recv_sem=sem_a1.at[1, p],
                device_id=(t, b), device_id_type=MESH,
            ).start()

        to_lev(p, 1, lambda t: xbuf.at[p, :, 1, t], rb.at[p, b], sem_b1)

        @pl.when(core == 1)
        def _():
            local(p, 2).start()

    def send2(p):
        local(p, 0).wait()
        wait_bytes(ra.at[p, pl.ds(0, SETS - 1)], sem_a1.at[1, p])

        @pl.when(core == 0)
        def _():
            local(p, 1).start()

        to_lev(p, 0, lambda t: ra.at[p, :, t], dbuf.at[p, b], sem_a2)

        @pl.when(core == 1)
        def _():
            local(p, 2).wait()
            wait_bytes(rb.at[p, pl.ds(0, LEVS - 1)], sem_b1.at[1, p])
            local(p, 3).start()

            for i in range(1, SETS):
                t = nth_set(i)
                pltpu.make_async_remote_copy(
                    src_ref=rb.at[p, :, t], dst_ref=dbuf.at[p, :, a],
                    send_sem=sem_b2.at[0, p], recv_sem=sem_b2.at[1, p], device_id=(t, b), device_id_type=MESH,
                ).start()

    def wait2(p):
        @pl.when(core == 0)
        def _():
            local(p, 1).wait()
            wait_bytes(dbuf.at[p, pl.ds(0, LEVS - 1)], sem_a2.at[1, p])

        @pl.when(core == 1)
        def _():
            local(p, 3).wait()
            wait_bytes(dbuf.at[p, :, pl.ds(0, SETS - 1)], sem_b2.at[1, p])

    def waits_of_sends(p):
        wait_bytes(ra.at[p, pl.ds(0, SETS - 1)], sem_a1.at[0, p])
        wait_sent_lev(p, 1, sem_b1)
        wait_sent_lev(p, 0, sem_a2)

        @pl.when(core == 1)
        def _():
            wait_bytes(dbuf.at[p, :, pl.ds(0, SETS - 1)], sem_b2.at[0, p])

    def legendre(p):
        m = wave[p]
        for c in load_spec(p):
            c.wait()
        @pl.when(p == 0)
        def _():
            load_ends.wait()

        for f in range(2):
            end = slast[f, p].reshape(2, 128).astype(F32)
            sbuf[f, p, 2560:2576] = jnp.concatenate([end, jnp.zeros((14, 128), F32)], axis=0).astype(BF16)

        @pl.loop(0, PAD // BLK, unroll=2)
        def _(t):
            j0 = pl.multiple_of(t * BLK, BLK)
            j = iota((2 * BLK, 128), 0) // 2 + j0
            degree = jnp.where(j <= TRUNC - m, m + j, j - 1)
            scale = (degree * (degree + 1)).astype(F32) * (1.0 / (TRUNC * (TRUNC + 1)))
            for f in range(2):
                x = sbuf[f, p, pl.ds(pl.multiple_of(2 * t * BLK, 2 * BLK), 2 * BLK), :]
                coupled = jnp.dot(x, vt[f], preferred_element_type=F32)
                adjf[f] = x.astype(F32) + scale * coupled
                for r in range(2):
                    abuf[pl.ds(j0, BLK), (2 * f + r) * 128 : (2 * f + r + 1) * 128] = adjf[
                        f, pl.ds(r, BLK, stride=2), :
                    ].astype(BF16)

        w_low = jnp.where(m == 0, 1.0, 2.0)
        jl = iota((256, HIGH0), 1) + HIGH0
        edge = tpt[:, HIGH0:1280].astype(F32)
        low_hi = jnp.where(jl <= TRUNC - m, edge * w_low, 0.0).astype(BF16)
        low = jnp.dot(
            (tpt[:, 0:HIGH0].astype(F32) * w_low).astype(BF16), abuf[0:HIGH0, :], preferred_element_type=F32
        )
        low = low + jnp.dot(low_hi, abuf[HIGH0:1280, :], preferred_element_type=F32)
        jh = iota((256, PAD - HIGH0), 1) + HIGH0
        keep = jnp.logical_and(jh > TRUNC - m, jh < ROWS)
        high_t = jnp.where(keep, tpt[:, HIGH0:PAD].astype(F32) * 2.0, 0.0).astype(BF16)
        high = jnp.dot(high_t, abuf[HIGH0:PAD, :], preferred_element_type=F32)
        band = jnp.concatenate([low.astype(BF16), high.astype(BF16)], axis=1)
        for q in range(4):
            placed = jnp.dot(band, place[:, q * 256 : q * 256 + 256], preferred_element_type=F32).astype(BF16)
            for e in range(2):
                for s in range(SETS):
                    xbuf[p, s, e, q] = placed[16 * s : 16 * s + 16, 128 * e : 128 * e + 128]

    def pass_waves():
        for e in range(2):
            pltpu.make_async_copy(
                wave_set.at[pl.ds(0, SETS - 1)], wave_set.at[pl.ds(0, SETS - 1)], sem_w1.at[e]
            ).wait()
        wave_set[a] = wave_me[...]
        packed = wave_set[:, 0, :]
        wave_pack[...] = packed
        wave_all[b] = packed

        @pl.loop(1, LEVS)
        def _(i):
            pltpu.make_async_remote_copy(
                src_ref=wave_pack, dst_ref=wave_all.at[b], send_sem=sem_w2.at[0], recv_sem=sem_w2.at[1],
                device_id=(a, nth_lev(i)), device_id_type=MESH,
            ).start()

    @pl.loop(0, PAIRS)
    def _(p):
        legendre(p)
        send1(p)

        @pl.when(p < PAIRS - 1)
        def _():
            turn_tables(p + 1)

        @pl.when(p == 1)
        def _():
            pass_waves()

        @pl.when(p >= 2)
        def _():
            send2(p - 2)

    for e in range(2):
        pltpu.make_async_copy(
            wave_all.at[pl.ds(0, LEVS - 1)], wave_all.at[pl.ds(0, LEVS - 1)], sem_w2.at[e]
        ).wait()

    wave_t[...] = wave_all[...].reshape(128, 128).T

    def tables(p):
        waves = wave_all[...].reshape(128, 128)
        mine = jnp.sum(jnp.where(iota((128, 128), 1) == p, waves, 0.0), axis=1, keepdims=True)
        m_all = jnp.broadcast_to(mine, (128, 128))
        wcol[...] = m_all
        sc, sn = turn(m_all * 128.0, clane[0:1, :], clane[1:2, :])
        m_row = jnp.broadcast_to(wave_t[pl.ds(p, 1), :], (8, 128))
        for h, waves_h in enumerate((m_row, TRUNC - m_row)):
            for t in range(1, LONS // SPAN):
                shift_c, shift_s = turn(waves_h * (SPAN * t), cval[...], cinv[...])
                shift[p, h, t, 0] = shift_c
                shift[p, h, t, 1] = shift_s
        step[0] = sc
        step[1] = sn

        @pl.loop(0, SLOTS, unroll=2)
        def _(s):
            count = cval[pl.ds(s, 1), :]
            inverse = cinv[pl.ds(s, 1), :]
            row = pl.multiple_of(p * 512, 512)
            pick_s = iota((32, 128), 1) == s
            for g in range(4):
                rows = slice(32 * g, 32 * g + 32)
                c, n = turn(wcol[rows, :] * iota((32, 128), 1).astype(F32), count, inverse)
                sc, sn = (
                    jnp.broadcast_to(
                        jnp.sum(jnp.where(pick_s, step[e, rows, :], 0.0), axis=1, keepdims=True), (32, 128)
                    )
                    for e in range(2)
                )
                for t in range(SPAN // 128):
                    cols = slice(128 * t, 128 * t + 128)
                    pc = psi_c[t, pl.ds(s, 1), :]
                    ps = psi_s[t, pl.ds(s, 1), :]
                    for e, v in enumerate((c, n, pc * c + ps * n, ps * c - pc * n)):
                        table[s, pl.ds(row + 128 * e + 32 * g, 32), cols] = v.astype(BF16)
                    if t < SPAN // 128 - 1:
                        c, n = c * sc - n * sn, n * sc + c * sn

    def gather(p):
        wait2(p)
        df[...] = dbuf[p].reshape(2048, 128).astype(F32)

        @pl.loop(0, SLOTS, unroll=4)
        def _(s):
            c0 = pl.multiple_of(p * 512, 512)
            for k in range(2):
                x = df[pl.ds(k * 8 + s, 128, stride=16), :].T
                for t in range(LONS // SPAN):
                    for h in range(2):
                        re, im = x[64 * h : 64 * h + 32], x[64 * h + 32 : 64 * h + 64]
                        if t > 0:
                            tc = shift[p, h, t, 0, pl.ds(s, 1), :]
                            ts = shift[p, h, t, 1, pl.ds(s, 1), :]
                            re, im = re * tc - im * ts, re * ts + im * tc
                        row = 64 * t + 32 * k
                        for e, v in enumerate((re, -im)):
                            at = pl.multiple_of(c0 + 256 * h + 128 * e, 128)
                            lhs[s, row : row + 32, pl.ds(at, 128)] = v.astype(BF16)

    FIRST = 512 * (PAIRS - 1)

    @pl.loop(0, PAIRS)
    def _(p):
        tables(p)

        @pl.when(p < 2)
        def _():
            send2(p + 3)

        @pl.when(p >= 2)
        def _():
            gather(p - 2)

    gather(3)

    @pl.loop(0, SLOTS, unroll=4)
    def _(s):
        acc[s] = jnp.dot(lhs[s, :, 0:FIRST], table[s, 0:FIRST, :], preferred_element_type=F32)

    gather(4)

    @pl.loop(0, SLOTS, unroll=4)
    def _(s):
        count = jnp.concatenate([cval[pl.ds(s, 1), :]] * 2, axis=1)
        total = acc[s] + jnp.dot(
            lhs[s, :, FIRST : 512 * PAIRS], table[s, FIRST : 512 * PAIRS, :], preferred_element_type=F32
        )
        for t in range(LONS // SPAN):
            lon = (iota((64, 256), 1) + SPAN * t).astype(F32)
            o = jnp.where(lon < count, total[64 * t : 64 * t + 64], 0.0)
            for e in range(2):
                outf[2 * t + e, pl.ds(s, 64, stride=8), :] = o[:, 128 * e : 128 * e + 128]

    for t in range(8):
        outb[:, :, :, :, 128 * t : 128 * t + 128] = outf[t].reshape(2, 2, 16, 8, 128).astype(BF16)
    done = [
        pltpu.make_async_copy(outb.at[0], out_f, sem_out.at[0]),
        pltpu.make_async_copy(outb.at[1], out_s, sem_out.at[1]),
    ]
    for c in done:
        c.start()

    @pl.loop(0, PAIRS)
    def _(p):
        waits_of_sends(p)

    for c in done:
        c.wait()


def hand_over(in_f, in_s, out_f, out_s, held, sems):
    parts = [(n, f, h) for n in range(2) for f in range(2) for h in range(2)]

    def come(n, f, h):
        src = (in_f, in_s)[n].at[f, pl.ds(8 * h, 8)]
        return pltpu.make_async_copy(src, held.at[n, f, pl.ds(8 * h, 8)], sems.at[0, n, f, h])

    def go(n, f, h):
        dst = (out_f, out_s)[n].at[f, pl.ds(8 * h, 8)]
        return pltpu.make_async_copy(held.at[n, f, pl.ds(8 * h, 8)], dst, sems.at[1, n, f, h])

    for part in parts:
        come(*part).start()
    for part in parts:
        come(*part).wait()
        go(*part).start()
    for part in parts:
        go(*part).wait()


def body(spectral, vertical, value_table, slope_table, wave_low, lat_slot, lon_counts):
    rows_first = jnp.transpose(spectral, (0, 3, 4, 2, 1))
    anywhere = pl.BlockSpec(memory_space=pl.ANY)
    scalars = pl.BlockSpec(memory_space=pltpu.SMEM)
    dma = pltpu.SemaphoreType.DMA
    out = jax.ShapeDtypeStruct((2, 16, SLOTS, LONS), BF16)
    gridded = pl.pallas_call(
        kernel,
        out_shape=(out, out),
        in_specs=[anywhere] * 4 + [scalars] * 3 + [pl.BlockSpec(memory_space=pltpu.VMEM)],
        out_specs=(anywhere, anywhere),
        scratch_shapes=[
            pltpu.VMEM((2, PAIRS, 2 * PAD, 128), BF16),
            pltpu.VMEM((2, PAIRS, 1, 2, 128), BF16),
            pltpu.VMEM((2, PAIRS, ROWS, 128), BF16),
            pltpu.VMEM((256, PAD), BF16),
            pltpu.VMEM((1024, 1024), BF16),
            pltpu.VMEM((PAD, 512), BF16),
            pltpu.VMEM((2, 2 * BLK, 128), F32),
            pltpu.VMEM((PAIRS, SETS, 2, 4, 16, 128), BF16),
            pltpu.VMEM((PAIRS, SETS, 4, 16, 128), BF16),
            pltpu.VMEM((PAIRS, LEVS, SETS, 16, 128), BF16),
            pltpu.VMEM((PAIRS, LEVS, SETS, 16, 128), BF16),
            pltpu.VMEM((LEVS, 2, 16, 128), BF16),
            pltpu.VMEM((2, 128, 128), BF16),
            pltpu.VMEM((8, 128), F32),
            pltpu.VMEM((SETS, 8, 128), F32),
            pltpu.VMEM((SETS, 128), F32),
            pltpu.VMEM((LEVS, SETS, 128), F32),
            pltpu.VMEM((128, 128), F32),
            pltpu.VMEM((128, 128), F32),
            pltpu.VMEM((PAIRS, 2, LONS // SPAN, 2, 8, 128), F32),
            pltpu.VMEM((2, 128, 128), F32),
            pltpu.VMEM((8, 128), F32),
            pltpu.VMEM((8, 128), F32),
            pltpu.VMEM((8, 128), F32),
            pltpu.VMEM((SPAN // 128, 8, 128), F32),
            pltpu.VMEM((SPAN // 128, 8, 128), F32),
            pltpu.VMEM((SLOTS, PAIRS * 512, SPAN), BF16),
            pltpu.VMEM((SLOTS, 256, PAIRS * 512), BF16),
            pltpu.VMEM((SLOTS, 256, SPAN), F32),
            pltpu.VMEM((2048, 128), F32),
            pltpu.VMEM((8, 512, 128), F32),
            pltpu.VMEM((2, 2, 16, SLOTS, LONS), BF16),
            dma((3, PAIRS)),
            dma((2, PAIRS)),
            dma((3,)),
            dma((2,)),
            dma((2,)),
            dma((2, PAIRS)),
            dma((2, PAIRS)),
            dma((2, PAIRS)),
            dma((2, PAIRS)),
            dma((4, PAIRS)),
            dma((2,)),
        ],
        compiler_params=pltpu.CompilerParams(
            collective_id=0, has_side_effects=True, vmem_limit_bytes=62 * 2**20
        ),
    )(
        rows_first, vertical, value_table, slope_table, wave_low, lat_slot, lon_counts,
        lat_slot.reshape(1, 128),
    )
    return pl.pallas_call(
        hand_over,
        out_shape=(out, out),
        in_specs=[anywhere] * 2,
        out_specs=(anywhere, anywhere),
        scratch_shapes=[pltpu.VMEM((2, 2, 16, SLOTS, LONS), BF16), dma((2, 2, 2, 2))],
    )(*gridded)


def solution(mesh):
    placed = (
        P(None, None, None, ("set", "lev"), None),
        P(None, "lev", None),
        P(("set", "lev"), None, None),
        P(("set", "lev"), None, None),
        P(("set", "lev")),
        P(),
        P(),
    )
    return jax.shard_map(
        body,
        mesh=mesh,
        in_specs=placed,
        out_specs=(P(None, "lev", "set", None), P(None, "lev", "set", None)),
        check_vma=False,
    )
```
